512 devices in a mesh: tm: 128 (over y, x_hi, z), head: 4 (over x_lo, core).
Axes of the slice: x: 4 (x_hi: 2, x_lo: 2; x = x_hi * 2 + x_lo), y: 8, z: 8, core: 2. Of those that a mesh axis runs over, the one named last changes fastest.
Arguments:
- hidden_states: bfloat16 [16384, 1280], P('tm', 'head'), may hold values from -24 to 24
- w_query: bfloat16 [1280, 1280], P(None, 'head'), may hold values from -1 to 1, as said below
- w_key: bfloat16 [1280, 1280], P(None, 'head'), may hold values from -1 to 1, as said below
- w_value: bfloat16 [1280, 1280], P(None, 'head'), may hold values from -0.15625 to 0.15625
- grad_out: bfloat16 [16384, 1280], P('tm', 'head'), may hold values from -6 to 6
Outputs:
- attended: bfloat16 [16384, 1280], P('tm', 'head')
- grad_query_weight: bfloat16 [1280, 1280], P(None, 'head')
- grad_hidden: bfloat16 [16384, 1280], P('tm', 'head')
The draws below stay inside these ranges and needn't reach their ends.
Inputs may be any that keep to these rules, and one draw needn't show every extreme that they name: `w_query`: entries of order 1280 ** -0.5. `w_key`: entries of order 1280 ** -0.5.
All inputs are finite; a program needn't handle non-finite values.
Results may differ from the reference program's by a relative error of at most 0.018.
Values may be sent and summed in bfloat16 or wider, within the bound.
A program may use at most 128 MiB of HBM per device.

```python
import jax
import jax.numpy as jnp
from jax import lax

C = 1280
HEADS = 20
P_SIZE = 64
CLIP = 8
HD = 64
FRAMES = 256


def shared_weight(key):
    return jnp.clip(jax.random.normal(key, (C, C), jnp.float32), -5.0, 5.0) * C ** (-0.5)


def draw_hidden_states(key, part):
    key = jax.random.fold_in(key, 11)
    base_key = jax.random.fold_in(key, 0)
    values = jnp.clip(jax.random.normal(base_key, (FRAMES * P_SIZE, C), jnp.float32), -6.0, 6.0)
    return values.astype(jnp.bfloat16)


def draw_w_query(key, part):
    return shared_weight(key).astype(jnp.bfloat16)


def draw_w_key(key, part):
    key = jax.random.fold_in(key, 23)
    own = shared_weight(key)
    values = own
    return values.astype(jnp.bfloat16)


def block_levels(stream_key, extent, pieces, low, largest):
    gain, own = 1.0, jax.random.fold_in(stream_key, 6)
    for position, shards_of in pieces:
        steps = jnp.exp(jax.random.uniform(jax.random.fold_in(own, position), (shards_of,), jnp.float32, low / len(pieces), largest / len(pieces)))
        gain = gain * jnp.repeat(steps, extent[position] // shards_of).reshape([-1 if axis == position else 1 for axis in range(len(extent))])
    return gain


def bell_draw(own_key, extent, scale, reach, cuts=(), kind=jnp.bfloat16):
    drawn = scale * jax.random.normal(own_key, extent, jnp.float32)
    if cuts:
        drawn = drawn * block_levels(own_key, extent, cuts, -0.22, 0.18)
    return jnp.clip(drawn, -reach, reach).astype(kind)


def setup_inputs(seed: int = 0) -> dict:
    seeds = jax.random.split(jax.random.key(seed), 6)
    return {
        "hidden_states": draw_hidden_states(jax.random.fold_in(seeds[5], 71), 0),
        "w_query": draw_w_query(jax.random.fold_in(seeds[5], 71), 0),
        "w_key": draw_w_key(jax.random.fold_in(seeds[5], 71), 0),
        "w_value": bell_draw(seeds[3], (C, C), C ** -0.5, 0.15625, ((1, 4),)),
        "grad_out": bell_draw(seeds[4], (FRAMES * P_SIZE, C), 1.0, 6.0, ((0, 128), (1, 4))),
    }


def project(rows, weight):
    return jnp.dot(rows, weight, preferred_element_type=jnp.float32).astype(jnp.bfloat16)


def reference(hidden_states, w_query, w_key, w_value, grad_out):
    scale = HD ** -0.5
    query = project(hidden_states, w_query).reshape(FRAMES, P_SIZE, HEADS, HD)
    key = project(hidden_states, w_key).reshape(FRAMES, P_SIZE, HEADS, HD)
    value = project(hidden_states, w_value).reshape(FRAMES, P_SIZE, HEADS, HD)
    cotan = grad_out.reshape(FRAMES, P_SIZE, HEADS, HD)

    def one_frame(frame):
        start = (frame - frame % CLIP).astype(jnp.int32)
        before = jnp.maximum(frame - 1, start).astype(jnp.int32)
        keys = jnp.concatenate([key[start], key[before]], 0).astype(jnp.float32)
        values = jnp.concatenate([value[start], value[before]], 0).astype(jnp.float32)
        own_query = query[frame].astype(jnp.float32)
        own_cotan = cotan[frame].astype(jnp.float32)
        scores = jnp.einsum('qhd,khd->hqk', own_query, keys) * scale
        probs = jax.nn.softmax(scores, axis=-1)
        probs_b = probs.astype(jnp.bfloat16).astype(jnp.float32)
        attended = jnp.einsum('hqk,khd->qhd', probs_b, values).astype(jnp.bfloat16)
        dprobs = jnp.einsum('qhd,khd->hqk', own_cotan, values)
        dscores = probs * (dprobs - jnp.sum(probs * dprobs, -1, keepdims=True)) * scale
        dscores_b = dscores.astype(jnp.bfloat16).astype(jnp.float32)
        dquery = jnp.einsum('hqk,khd->qhd', dscores_b, keys).astype(jnp.bfloat16)
        dkeys = jnp.einsum('hqk,qhd->khd', dscores_b, own_query)
        dvalues = jnp.einsum('hqk,qhd->khd', probs_b, own_cotan)
        return attended, dquery, dkeys, dvalues

    attended, dquery, dkeys, dvalues = lax.map(one_frame, jnp.arange(FRAMES, dtype=jnp.int32))

    def totals(parts):
        parts = parts.reshape((FRAMES // CLIP, CLIP) + parts.shape[1:])
        anchor = jnp.sum(parts[:, :, :P_SIZE], axis=1)
        before = parts[:, :, P_SIZE:]
        moved = jnp.concatenate([before[:, 1:], jnp.zeros_like(before[:, :1])], 1)
        moved = moved.at[:, 0].add(anchor + before[:, 0])
        return moved.reshape((FRAMES,) + moved.shape[2:])

    dkey = totals(dkeys).astype(jnp.bfloat16).reshape(FRAMES * P_SIZE, C)
    dvalue = totals(dvalues).astype(jnp.bfloat16).reshape(FRAMES * P_SIZE, C)
    dquery = dquery.reshape(FRAMES * P_SIZE, C)
    grad_weight = jnp.dot(hidden_states.T, dquery, preferred_element_type=jnp.float32).astype(jnp.bfloat16)
    grad_hidden = jnp.dot(dquery, w_query.T, preferred_element_type=jnp.float32)
    grad_hidden = grad_hidden + jnp.dot(dkey, w_key.T, preferred_element_type=jnp.float32)
    grad_hidden = grad_hidden + jnp.dot(dvalue, w_value.T, preferred_element_type=jnp.float32)
    return attended.reshape(FRAMES * P_SIZE, C), grad_weight, grad_hidden.astype(jnp.bfloat16)
```

```python
import functools

import jax
import jax.numpy as jnp
from jax import lax
from jax.experimental import pallas as pl
from jax.experimental.pallas import tpu as pltpu
from jax.sharding import PartitionSpec as P

MESH = pl.DeviceIdType.MESH
F32 = jnp.float32
BF16 = jnp.bfloat16

P_SIZE = 64
HD = 64
SPAN = 4
NZ = 8
GROUP = 8
CROSS = 16
HEADS_AX = 4
WIN = 384
NT = (((1,), (1,)), ((), ()))


def mm(a, b):
    return jnp.dot(a, b, preferred_element_type=F32)


def mm_nt(a, b):
    return lax.dot_general(a, b, NT, preferred_element_type=F32)


def roll_half(x):
    return pltpu.roll(x, P_SIZE, 1)


def low_lanes(shape):
    return lax.broadcasted_iota(jnp.int32, shape, 1) < P_SIZE


def pack(tile, half):
    n = tile.shape[0] // 2
    top, bottom = tile[:n], tile[n:]
    low = low_lanes((n, 128))
    if half == 0:
        return jnp.where(low, top, roll_half(bottom))
    return jnp.where(low, roll_half(top), bottom)


def unpack(first, second):
    low = low_lanes(first.shape)
    return jnp.concatenate(
        [jnp.where(low, first, roll_half(second)), jnp.where(low, roll_half(first), second)], 0
    )


def kernel(
    hid_ref, wq_ref, wk_ref, wv_ref, go_ref,
    att_ref, gw_ref, gh_ref,
    xt, et, wt, gt, pk_lo, pk_hi, in_lo, in_hi,
    qkv, kve, kvn, dqt, fall, dqall, part, parts_in, small, yt, gh_in, pg_lo, pg_hi, gin_lo, gin_hi,
    pts, local_sem, a1_s, a1_r, a2_s, a2_r, a3_s, a3_r, fe_s, fe_r, c_s, c_r,
    e_s, e_r, f_s, f_r, g_s, g_r, h_s, h_r, z_s, z_r,
):
    tm = lax.axis_index("tm")
    head = lax.axis_index("head")
    core = head % 2
    z = tm % NZ
    xh = (tm // NZ) % 2
    y = tm // (2 * NZ)
    place = z % SPAN
    pos = (1 - core) * z + core * y
    stride = (1 - core) + core * 2 * NZ
    pos2 = (1 - core) * y + core * z
    stride2 = (1 - core) * 2 * NZ + core
    cross = pos2 * 2 + xh
    width = hid_ref.shape[0]
    half_w = width // 2

    def copy(src, dst, send, recv, device):
        return pltpu.make_async_remote_copy(
            src_ref=src, dst_ref=dst, send_sem=send, recv_sem=recv,
            device_id=device, device_id_type=MESH,
        )

    def head_peer(r):
        return (tm, (head + r) % HEADS_AX)

    def group_pos(r):
        return (pos + r) % GROUP

    def group_peer(r):
        return (tm + (group_pos(r) - pos) * stride, head)

    def cross_pos(r):
        return (cross + r) % CROSS

    def cross_peer(r):
        k = cross_pos(r)
        return (tm + (k // 2 - pos2) * stride2 + (k % 2 - xh) * NZ, head)

    def head_rows(h):
        return pl.ds(pl.multiple_of(h * width, 64), width)

    def win_start(j):
        a = j // 2
        return pl.multiple_of(640 * (a // 2) + 256 * (a % 2), 128)

    def win_rows(j):
        return pl.multiple_of((j % 2) * half_w, 32)

    own_x = xt.at[head_rows(head)]
    loads = [
        pltpu.make_async_copy(hid_ref, own_x, local_sem.at[0]),
        pltpu.make_async_copy(wq_ref, wt.at[pl.ds(0, width)], local_sem.at[1]),
        pltpu.make_async_copy(wk_ref, wt.at[pl.ds(width, width)], local_sem.at[2]),
        pltpu.make_async_copy(wv_ref, wt.at[pl.ds(2 * width, width)], local_sem.at[3]),
        pltpu.make_async_copy(go_ref, gt, local_sem.at[4]),
    ]
    for load in loads:
        load.start()

    barrier = pltpu.get_barrier_semaphore()
    peers = (
        [head_peer(r) for r in range(1, HEADS_AX)]
        + [group_peer(r) for r in range(1, GROUP)]
        + [cross_peer(r) for r in range(1, CROSS)]
    )
    for peer in peers:
        pl.semaphore_signal(barrier, inc=1, device_id=peer, device_id_type=MESH)
    loads[0].wait()
    tile = xt[head_rows(head), :].astype(F32)
    pk_lo[...] = pack(tile, 0).astype(BF16)
    pk_hi[...] = pack(tile, 1).astype(BF16)
    pl.semaphore_wait(barrier, len(peers))

    def a1(r):
        return copy(own_x, own_x, a1_s.at[r - 1], a1_r.at[r - 1], head_peer(r))

    def a1_in(r):
        rows = xt.at[head_rows((head - r + HEADS_AX) % HEADS_AX)]
        return copy(rows, rows, a1_s.at[r - 1], a1_r.at[r - 1], head_peer(r))

    for r in range(1, HEADS_AX):
        a1(r).start()

    def lead_out(p):
        return copy(pk_lo, in_lo, a2_s.at[p - 1], a2_r.at[0], (tm + p, head))

    def prev_out():
        return copy(pk_hi, in_hi, a2_s.at[3], a2_r.at[1], (tm + 1, head))

    @pl.when(place == 0)
    def _():
        for p in range(1, SPAN):
            lead_out(p).start()

    @pl.when(place < SPAN - 1)
    def _():
        prev_out().start()

    own_e = et.at[head_rows(head)]

    @pl.when(place == 0)
    def _():
        et[head_rows(head), :] = jnp.where(low_lanes(tile.shape), tile, roll_half(tile)).astype(BF16)

    @pl.when(place > 0)
    def _():
        copy(pk_lo, in_lo, a2_s.at[0], a2_r.at[0], (tm, (head + 1) % HEADS_AX)).wait_recv()
        copy(pk_hi, in_hi, a2_s.at[3], a2_r.at[1], (tm, (head + 1) % HEADS_AX)).wait_recv()
        et[head_rows(head), :] = unpack(in_lo[...].astype(F32), in_hi[...].astype(F32)).astype(BF16)

    def a3(r):
        return copy(own_e, own_e, a3_s.at[r - 1], a3_r.at[r - 1], head_peer(r))

    def a3_in(r):
        rows = et.at[head_rows((head - r + HEADS_AX) % HEADS_AX)]
        return copy(rows, rows, a3_s.at[r - 1], a3_r.at[r - 1], head_peer(r))

    for r in range(1, HEADS_AX):
        a3(r).start()
    for r in range(1, HEADS_AX):
        a1_in(r).wait_recv()

    def fe(r):
        return copy(
            xt.at[pl.ds(win_start(group_pos(r)), WIN)], fall.at[:, pl.ds(128 * r, 128)],
            fe_s.at[r - 1], fe_r.at[r - 1], group_peer(r),
        )

    for r in range(1, GROUP):
        fe(r).start()
    fall[:, 0:128] = xt[pl.ds(win_start(pos), WIN), :]

    for load in loads[1:]:
        load.wait()
    qkv[...] = mm(wt[...], xt[...]).astype(BF16)
    kvn[1] = jnp.transpose(qkv[width:, :])
    for r in range(1, HEADS_AX):
        a3_in(r).wait_recv()
    kve[...] = mm(wt[width:, :], et[...]).astype(BF16)
    kvn[0] = jnp.transpose(kve[...])

    scale = HD ** (-0.5)
    low = low_lanes((P_SIZE, 128))
    zero = jnp.zeros((P_SIZE, 128), BF16)
    heads_here = width // HD

    def spread(lead, second, index):
        pts[index, 0:64, :] = lead
        pts[index, 64:128, :] = jnp.where(low, second, zero)
        pts[index, 128:192, :] = jnp.where(low, zero, second)
        pts[index, 192:256, :] = zero

    for i in range(heads_here):
        a, b = HD * i, HD * (i + 1)
        q = qkv[a:b, :]
        cot = gt[a:b, :]
        k_extra, k_own = kvn[0, :, a:b], kvn[1, 0:64, a:b]
        v_extra, v_own = kvn[0, :, width + a : width + b], kvn[1, 0:64, width + a : width + b]
        s_extra, s_own = mm(k_extra, q) * scale, mm(k_own, q) * scale
        s_lead, s_second = s_extra[:64], jnp.where(low, s_extra[64:], s_own)
        top = jnp.maximum(
            jnp.max(s_lead, 0, keepdims=True), jnp.max(s_second, 0, keepdims=True)
        )
        e_lead, e_second = jnp.exp(s_lead - top), jnp.exp(s_second - top)
        inv = 1.0 / (jnp.sum(e_lead, 0, keepdims=True) + jnp.sum(e_second, 0, keepdims=True))
        p_lead, p_second = e_lead * inv, e_second * inv
        d_extra, d_own = mm(v_extra, cot), mm(v_own, cot)
        d_lead, d_second = d_extra[:64], jnp.where(low, d_extra[64:], d_own)
        inner = jnp.sum(p_lead * d_lead, 0, keepdims=True) + jnp.sum(
            p_second * d_second, 0, keepdims=True
        )
        spread(
            (p_lead * (d_lead - inner) * scale).astype(BF16),
            (p_second * (d_second - inner) * scale).astype(BF16),
            2 * i,
        )
        spread(p_lead.astype(BF16), p_second.astype(BF16), 2 * i + 1)
        k_wide = jnp.concatenate([kve[a:b, :], qkv[width + a : width + b, :]], 1)
        dqt[a:b, :] = mm(k_wide, pts[2 * i]).astype(BF16)

    def cc(r):
        return copy(
            dqt.at[pl.ds(win_rows(group_pos(r)), half_w)], dqall.at[:, pl.ds(128 * r, 128)],
            c_s.at[r - 1], c_r.at[r - 1], group_peer(r),
        )

    for r in range(1, GROUP):
        cc(r).start()
    dqall[:, 0:128] = dqt[pl.ds(win_rows(pos), half_w), :]

    dks, dvs = [], []
    for i in range(heads_here):
        a, b = HD * i, HD * (i + 1)
        v_wide = jnp.concatenate(
            [kve[width + a : width + b, :], qkv[2 * width + a : 2 * width + b, :]], 1
        )
        att_ref[a:b, :] = mm(v_wide, pts[2 * i + 1]).astype(BF16)
        dks.append(mm_nt(qkv[a:b, :], pts[2 * i]).astype(BF16))
        dvs.append(mm_nt(gt[a:b, :], pts[2 * i + 1]).astype(BF16))

    dk_n = jnp.transpose(jnp.concatenate(dks, 0))
    dv_n = jnp.transpose(jnp.concatenate(dvs, 0))
    dq_n = jnp.transpose(dqt[...])
    for c in range(5):
        cols = slice(256 * c, 256 * (c + 1))
        terms = mm(dk_n, wt[width : 2 * width, cols]) + mm(dv_n, wt[2 * width :, cols])
        own = terms[128:] + mm(dq_n, wt[0:width, cols])
        yt[cols, 0:128] = jnp.transpose(terms[:128].astype(BF16))
        yt[cols, 128:256] = jnp.transpose(own.astype(BF16))

    def hh(r):
        return copy(
            yt.at[head_rows((head + r) % HEADS_AX)], gh_in.at[r - 1],
            h_s.at[r - 1], h_r.at[r - 1], head_peer(r),
        )

    for r in range(1, HEADS_AX):
        hh(r).start()

    for r in range(1, GROUP):
        fe(r).wait_recv()
    for r in range(1, GROUP):
        cc(r).wait_recv()
    window = mm_nt(dqall[...], fall[...]).astype(BF16)
    for k in range(15):
        i, l = k // 3, k % 3
        part[k] = window[32 * i : 32 * i + 32, 128 * l : 128 * l + 128]
    part[15] = jnp.zeros((32, 128), BF16)

    def ee(r):
        return copy(
            part.at[cross_pos(r)], parts_in.at[r - 1], e_s.at[r - 1], e_r.at[r - 1], cross_peer(r)
        )

    for r in range(1, CROSS):
        ee(r).start()
    for r in range(1, CROSS):
        ee(r).wait_recv()
    total = part[cross].astype(F32)
    for r in range(1, CROSS):
        total = total + parts_in[r - 1].astype(F32)

    even = (pos // 2) % 2 == 0

    def piece(k):
        return gw_ref.at[
            pl.ds(pl.multiple_of(win_rows(pos) + 32 * (k // 3), 32), 32),
            pl.ds(pl.multiple_of(win_start(pos) + 128 * (k % 3), 128), 128),
        ]

    def holds(k):
        return (k < 15) & (even | (k % 3 > 0))

    def ff(r):
        return copy(piece(cross), piece(cross), f_s.at[r - 1], f_r.at[r - 1], cross_peer(r))

    def ff_in(r):
        k = (cross - r + CROSS) % CROSS
        return k, copy(piece(k), piece(k), f_s.at[r - 1], f_r.at[r - 1], cross_peer(r))

    @pl.when(holds(cross))
    def _():
        gw_ref[
            pl.ds(pl.multiple_of(win_rows(pos) + 32 * (cross // 3), 32), 32),
            pl.ds(pl.multiple_of(win_start(pos) + 128 * (cross % 3), 128), 128),
        ] = total.astype(BF16)
        for r in range(1, CROSS):
            ff(r).start()

    for r in range(1, HEADS_AX):
        hh(r).wait_recv()
    summed = yt[head_rows(head), :].astype(F32)
    for r in range(1, HEADS_AX):
        summed = summed + gh_in[r - 1].astype(F32)
    extra, own = summed[:, :128], summed[:, 128:]
    pg_lo[...] = pack(extra, 0).astype(BF16)
    pg_hi[...] = pack(extra, 1).astype(BF16)

    def lead_back(p):
        return copy(pg_lo, gin_lo.at[p - 1], z_s.at[0], z_r.at[p - 1], (tm - p, head))

    def prev_back():
        return copy(pg_hi, gin_hi, z_s.at[1], z_r.at[3], (tm - 1, head))

    for p in range(1, SPAN):
        @pl.when(place == p)
        def _(p=p):
            lead_back(p).start()
            prev_back().start()

    for r in range(1, CROSS):
        k, arrival = ff_in(r)

        @pl.when(holds(k))
        def _(arrival=arrival):
            arrival.wait_recv()

    def wide(j):
        return gw_ref.at[
            pl.ds(win_rows(j), half_w), pl.ds(pl.multiple_of(win_start(j) + 128, 128), 256)
        ]

    def slim(j):
        return gw_ref.at[pl.ds(win_rows(j), half_w), pl.ds(win_start(j), 128)]

    def gg(r, j, region, slot):
        return copy(
            region(j), region(j), g_s.at[slot, r - 1], g_r.at[slot, r - 1], group_peer(r)
        )

    for r in range(1, GROUP):
        gg(r, pos, wide, 0).start()

        @pl.when(even)
        def _(r=r):
            gg(r, pos, slim, 1).start()

    low_tile = low_lanes(own.shape)

    @pl.when(place == 0)
    def _():
        for p in range(1, SPAN):
            copy(pg_lo, gin_lo.at[p - 1], z_s.at[0], z_r.at[p - 1], (tm, (head + 1) % HEADS_AX)).wait_recv()

    @pl.when(place < SPAN - 1)
    def _():
        copy(pg_hi, gin_hi, z_s.at[1], z_r.at[3], (tm, (head + 1) % HEADS_AX)).wait_recv()

    lead_sum = gin_lo[0].astype(F32) + gin_lo[1].astype(F32) + gin_lo[2].astype(F32)
    lead_sum = jnp.where(place == 0, lead_sum, 0.0)
    prev_in = jnp.where(place < SPAN - 1, gin_hi[...].astype(F32), 0.0)
    local = jnp.where((place == 0) & low_tile, extra + roll_half(extra), 0.0)
    gh_ref[...] = (own + local + unpack(lead_sum, prev_in)).astype(BF16)

    for r in range(1, GROUP):
        j = (pos - r + GROUP) % GROUP
        gg(r, j, wide, 0).wait_recv()

        @pl.when((j // 2) % 2 == 0)
        def _(r=r, j=j):
            gg(r, j, slim, 1).wait_recv()

    for r in range(1, HEADS_AX):
        a1(r).wait_send()
        a3(r).wait_send()
        hh(r).wait_send()

    @pl.when(place == 0)
    def _():
        for p in range(1, SPAN):
            lead_out(p).wait_send()

    @pl.when(place < SPAN - 1)
    def _():
        prev_out().wait_send()

    @pl.when(place > 0)
    def _():
        lead_back(1).wait_send()
        prev_back().wait_send()

    for r in range(1, GROUP):
        fe(r).wait_send()
        cc(r).wait_send()
        gg(r, pos, wide, 0).wait_send()

    @pl.when(even)
    def _():
        for r in range(1, GROUP):
            gg(r, pos, slim, 1).wait_send()

    for r in range(1, CROSS):
        ee(r).wait_send()

    @pl.when(holds(cross))
    def _():
        for r in range(1, CROSS):
            ff(r).wait_send()


def shards(hidden_states, w_query, w_key, w_value, grad_out):
    rows, width = hidden_states.shape
    full = w_query.shape[0]
    half = width // 2
    vm = pltpu.VMEM
    dma = pltpu.SemaphoreType.DMA
    scratch = [
        vm((full, rows), BF16),
        vm((full, rows), BF16),
        vm((3 * width, full), BF16),
        vm((width, rows), BF16),
        vm((half, 128), BF16), vm((half, 128), BF16),
        vm((half, 128), BF16), vm((half, 128), BF16),
        vm((3 * width, rows), BF16),
        vm((2 * width, rows), BF16),
        vm((2, rows, 2 * width), BF16),
        vm((width, rows), BF16),
        vm((WIN, GROUP * 128), BF16),
        vm((half, GROUP * 128), BF16),
        vm((CROSS, 32, 128), BF16),
        vm((CROSS - 1, 32, 128), BF16),
        vm((8, 128), F32),
        vm((full, 256), BF16),
        vm((HEADS_AX - 1, width, 256), BF16),
        vm((half, 128), BF16), vm((half, 128), BF16),
        vm((SPAN - 1, half, 128), BF16), vm((half, 128), BF16),
        vm((2 * (width // HD), 256, 128), BF16),
        dma((5,)),
        dma((3,)), dma((3,)),
        dma((4,)), dma((2,)),
        dma((3,)), dma((3,)),
        dma((GROUP - 1,)), dma((GROUP - 1,)),
        dma((GROUP - 1,)), dma((GROUP - 1,)),
        dma((CROSS - 1,)), dma((CROSS - 1,)),
        dma((CROSS - 1,)), dma((CROSS - 1,)),
        dma((2, GROUP - 1)), dma((2, GROUP - 1)),
        dma((3,)), dma((3,)),
        dma((2,)), dma((4,)),
    ]
    att, gw, gh = pl.pallas_call(
        kernel,
        out_shape=(
            jax.ShapeDtypeStruct((width, rows), BF16),
            jax.ShapeDtypeStruct((width, full), BF16),
            jax.ShapeDtypeStruct((width, rows), BF16),
        ),
        in_specs=[pl.BlockSpec(memory_space=pl.ANY)] * 5,
        out_specs=[pl.BlockSpec(memory_space=pltpu.VMEM)] * 3,
        scratch_shapes=scratch,
        compiler_params=pltpu.CompilerParams(
            collective_id=0, has_side_effects=True, vmem_limit_bytes=40 * 2**20
        ),
    )(hidden_states.T, w_query.T, w_key.T, w_value.T, grad_out.T)
    return att.T, gw.T, gh.T


def solution(mesh):
    placed = (P("tm", "head"), P(None, "head"), P(None, "head"), P(None, "head"), P("tm", "head"))
    return jax.shard_map(
        shards,
        mesh=mesh,
        in_specs=placed,
        out_specs=(P("tm", "head"), P(None, "head"), P("tm", "head")),
        check_vma=False,
    )
```

```python
import functools

import jax
import jax.numpy as jnp
from jax import lax
from jax.experimental import pallas as pl
from jax.experimental.pallas import tpu as pltpu
from jax.sharding import PartitionSpec as P

MESH = pl.DeviceIdType.MESH
F32 = jnp.float32
BF16 = jnp.bfloat16

P_SIZE = 64
HD = 64
SPAN = 4
NZ = 8
GROUP = 8
CROSS = 16
HEADS_AX = 4
FAR_FIRST = sorted(range(1, GROUP), key=lambda r: abs(r - GROUP // 2))
CROSS_FAR_FIRST = sorted(range(1, CROSS), key=lambda r: abs(r - CROSS // 2))
WIN = 384
NT = (((1,), (1,)), ((), ()))


def mm(a, b):
    return jnp.dot(a, b, preferred_element_type=F32)


def mm_nt(a, b):
    return lax.dot_general(a, b, NT, preferred_element_type=F32)


def roll_half(x):
    return pltpu.roll(x, P_SIZE, 1)


def low_lanes(shape):
    return lax.broadcasted_iota(jnp.int32, shape, 1) < P_SIZE


def pack(tile, half):
    n = tile.shape[0] // 2
    top, bottom = tile[:n], tile[n:]
    low = low_lanes((n, 128))
    if half == 0:
        return jnp.where(low, top, roll_half(bottom))
    return jnp.where(low, roll_half(top), bottom)


def unpack(first, second):
    low = low_lanes(first.shape)
    return jnp.concatenate(
        [jnp.where(low, first, roll_half(second)), jnp.where(low, roll_half(first), second)], 0
    )


def kernel(
    hid_ref, wq_ref, wk_ref, wv_ref, go_ref,
    att_ref, gw_ref, gh_ref,
    xt, et, wt, gt, pk_lo, pk_hi, in_lo, in_hi,
    qkv, kve, kvn, dqt, fall, dqall, part, parts_in, yt, gh_in, pg_lo, pg_hi, gin_lo, gin_hi,
    pts, local_sem, a1_s, a1_r, a2_s, a2_r, a3_s, a3_r, fe_s, fe_r, c_s, c_r,
    e_s, e_r, f_s, f_r, g_s, g_r, h_s, h_r, z_s, z_r,
):
    tm = lax.axis_index("tm")
    head = lax.axis_index("head")
    core = head % 2
    z = tm % NZ
    xh = (tm // NZ) % 2
    y = tm // (2 * NZ)
    place = z % SPAN
    pos = (1 - core) * z + core * y
    stride = (1 - core) + core * 2 * NZ
    pos2 = (1 - core) * y + core * z
    stride2 = (1 - core) * 2 * NZ + core
    cross = pos2 * 2 + xh
    width = hid_ref.shape[0]
    half_w = width // 2

    def copy(src, dst, send, recv, device):
        return pltpu.make_async_remote_copy(
            src_ref=src, dst_ref=dst, send_sem=send, recv_sem=recv,
            device_id=device, device_id_type=MESH,
        )

    def head_peer(r):
        return (tm, (head + r) % HEADS_AX)

    def group_pos(r):
        return (pos + r) % GROUP

    def group_peer(r):
        return (tm + (group_pos(r) - pos) * stride, head)

    def cross_pos(r):
        return (cross + r) % CROSS

    def cross_peer(r):
        k = cross_pos(r)
        return (tm + (k // 2 - pos2) * stride2 + (k % 2 - xh) * NZ, head)

    def head_rows(h):
        return pl.ds(pl.multiple_of(h * width, 64), width)

    def is_wide(j):
        return (j // 2) % 2 == 0

    def by_tiles(j, run):
        pl.when(is_wide(j))(lambda: run(3))
        pl.when(jnp.logical_not(is_wide(j)))(lambda: run(2))

    def win_start(j):
        a = j // 2
        return pl.multiple_of(640 * (a // 2) + 384 * (a % 2), 128)

    def win_rows(j):
        return pl.multiple_of((j % 2) * half_w, 32)

    barrier = pltpu.get_barrier_semaphore()
    peers = (
        [head_peer(r) for r in range(1, HEADS_AX)]
        + [group_peer(r) for r in range(1, GROUP)]
        + [cross_peer(r) for r in range(1, CROSS)]
    )
    for peer in peers:
        pl.semaphore_signal(barrier, inc=1, device_id=peer, device_id_type=MESH)

    own_x = xt.at[head_rows(head)]
    loads = [
        pltpu.make_async_copy(hid_ref, own_x, local_sem.at[0]),
        pltpu.make_async_copy(wq_ref, wt.at[pl.ds(0, width)], local_sem.at[1]),
        pltpu.make_async_copy(wk_ref, wt.at[pl.ds(width, width)], local_sem.at[2]),
        pltpu.make_async_copy(wv_ref, wt.at[pl.ds(2 * width, width)], local_sem.at[3]),
        pltpu.make_async_copy(go_ref, gt, local_sem.at[4]),
    ]
    for load in loads:
        load.start()
    loads[0].wait()
    tile = xt[head_rows(head), :].astype(F32)
    pk_lo[...] = pack(tile, 0).astype(BF16)
    pk_hi[...] = pack(tile, 1).astype(BF16)
    pl.semaphore_wait(barrier, len(peers))

    def a1(r):
        return copy(own_x, own_x, a1_s.at[r - 1], a1_r.at[r - 1], head_peer(r))

    def a1_in(r):
        rows = xt.at[head_rows((head - r + HEADS_AX) % HEADS_AX)]
        return copy(rows, rows, a1_s.at[r - 1], a1_r.at[r - 1], head_peer(r))

    for r in range(1, HEADS_AX):
        a1(r).start()

    def lead_out(p):
        return copy(pk_lo, in_lo, a2_s.at[p - 1], a2_r.at[0], (tm + p, head))

    def prev_out():
        return copy(pk_hi, in_hi, a2_s.at[3], a2_r.at[1], (tm + 1, head))

    @pl.when(place == 0)
    def _():
        for p in range(1, SPAN):
            lead_out(p).start()

    @pl.when(place < SPAN - 1)
    def _():
        prev_out().start()

    own_e = et.at[head_rows(head)]

    @pl.when(place == 0)
    def _():
        et[head_rows(head), :] = jnp.where(low_lanes(tile.shape), tile, roll_half(tile)).astype(BF16)

    @pl.when(place > 0)
    def _():
        copy(pk_lo, in_lo, a2_s.at[0], a2_r.at[0], (tm, (head + 1) % HEADS_AX)).wait_recv()
        copy(pk_hi, in_hi, a2_s.at[3], a2_r.at[1], (tm, (head + 1) % HEADS_AX)).wait_recv()
        et[head_rows(head), :] = unpack(in_lo[...].astype(F32), in_hi[...].astype(F32)).astype(BF16)

    def a3(r):
        return copy(own_e, own_e, a3_s.at[r - 1], a3_r.at[r - 1], head_peer(r))

    def a3_in(r):
        rows = et.at[head_rows((head - r + HEADS_AX) % HEADS_AX)]
        return copy(rows, rows, a3_s.at[r - 1], a3_r.at[r - 1], head_peer(r))

    for r in range(1, HEADS_AX):
        a3(r).start()
    for r in range(1, HEADS_AX):
        a1_in(r).wait_recv()

    def fe(r, j, tiles):
        return copy(
            xt.at[pl.ds(win_start(j), 128 * tiles)], fall.at[r, pl.ds(0, 128 * tiles)],
            fe_s.at[r - 1], fe_r.at[r - 1], group_peer(r),
        )

    for r in FAR_FIRST:
        by_tiles(group_pos(r), lambda tiles, r=r: fe(r, group_pos(r), tiles).start())

    @pl.when(is_wide(pos))
    def _():
        fall[0] = xt[pl.ds(win_start(pos), 384), :]

    @pl.when(jnp.logical_not(is_wide(pos)))
    def _():
        fall[0, 0:256] = xt[pl.ds(win_start(pos), 256), :]
        for r in range(GROUP):
            fall[r, 256:384] = jnp.zeros((128, 128), BF16)

    for load in loads[1:]:
        load.wait()
    qkv[...] = mm(wt[...], xt[...]).astype(BF16)
    kvn[1] = jnp.transpose(qkv[width:, :])
    for r in range(1, HEADS_AX):
        a3_in(r).wait_recv()
    kve[...] = mm(wt[width:, :], et[...]).astype(BF16)
    kvn[0] = jnp.transpose(kve[...])

    scale = HD ** (-0.5)
    low = low_lanes((P_SIZE, 128))
    zero = jnp.zeros((P_SIZE, 128), BF16)
    heads_here = width // HD

    def spread(lead, second, index):
        pts[index, 0:64, :] = lead
        pts[index, 64:128, :] = jnp.where(low, second, zero)
        pts[index, 128:192, :] = jnp.where(low, zero, second)
        pts[index, 192:256, :] = zero

    def cc(r):
        return copy(
            dqt.at[pl.ds(win_rows(group_pos(r)), half_w)], dqall.at[r],
            c_s.at[r - 1], c_r.at[r - 1], group_peer(r),
        )

    def send_half(part):
        for r in FAR_FIRST:
            pl.when(group_pos(r) % 2 == part)(lambda r=r: cc(r).start())

    for i in range(heads_here):
        a, b = HD * i, HD * (i + 1)
        q = qkv[a:b, :]
        cot = gt[a:b, :]
        k_extra, k_own = kvn[0, :, a:b], kvn[1, 0:64, a:b]
        v_extra, v_own = kvn[0, :, width + a : width + b], kvn[1, 0:64, width + a : width + b]
        s_extra, s_own = mm(k_extra, q) * scale, mm(k_own, q) * scale
        s_lead, s_second = s_extra[:64], jnp.where(low, s_extra[64:], s_own)
        top = jnp.maximum(
            jnp.max(s_lead, 0, keepdims=True), jnp.max(s_second, 0, keepdims=True)
        )
        e_lead, e_second = jnp.exp(s_lead - top), jnp.exp(s_second - top)
        inv = 1.0 / (jnp.sum(e_lead, 0, keepdims=True) + jnp.sum(e_second, 0, keepdims=True))
        p_lead, p_second = e_lead * inv, e_second * inv
        d_extra, d_own = mm(v_extra, cot), mm(v_own, cot)
        d_lead, d_second = d_extra[:64], jnp.where(low, d_extra[64:], d_own)
        inner = jnp.sum(p_lead * d_lead, 0, keepdims=True) + jnp.sum(
            p_second * d_second, 0, keepdims=True
        )
        spread(
            (p_lead * (d_lead - inner) * scale).astype(BF16),
            (p_second * (d_second - inner) * scale).astype(BF16),
            2 * i,
        )
        spread(p_lead.astype(BF16), p_second.astype(BF16), 2 * i + 1)
        k_wide = jnp.concatenate([kve[a:b, :], qkv[width + a : width + b, :]], 1)
        dqt[a:b, :] = mm(k_wide, pts[2 * i]).astype(BF16)
        if a < half_w <= b:
            send_half(0)
    send_half(1)
    dqall[0] = dqt[pl.ds(win_rows(pos), half_w), :]


    dks, dvs = [], []
    for i in range(heads_here):
        a, b = HD * i, HD * (i + 1)
        v_wide = jnp.concatenate(
            [kve[width + a : width + b, :], qkv[2 * width + a : 2 * width + b, :]], 1
        )
        att_ref[a:b, :] = mm(v_wide, pts[2 * i + 1]).astype(BF16)
        dks.append(mm_nt(qkv[a:b, :], pts[2 * i]).astype(BF16))
        dvs.append(mm_nt(gt[a:b, :], pts[2 * i + 1]).astype(BF16))

    for r in range(1, GROUP):
        by_tiles(pos, lambda tiles, r=r: fe(r, pos, tiles).wait_recv())
    for r in range(1, GROUP):
        cc(r).wait_recv()
    window = mm_nt(
        jnp.concatenate([dqall[r] for r in range(GROUP)], 1),
        jnp.concatenate([fall[r] for r in range(GROUP)], 1),
    ).astype(BF16)
    for k in range(15):
        i, l = k // 3, k % 3
        part[k] = window[32 * i : 32 * i + 32, 128 * l : 128 * l + 128]
    part[15] = jnp.zeros((32, 128), BF16)

    def ee(r):
        return copy(
            part.at[cross_pos(r)], parts_in.at[r - 1], e_s.at[r - 1], e_r.at[r - 1], cross_peer(r)
        )

    for r in CROSS_FAR_FIRST:
        ee(r).start()

    dk_n = jnp.transpose(jnp.concatenate(dks, 0))
    dv_n = jnp.transpose(jnp.concatenate(dvs, 0))
    dq_n = jnp.transpose(dqt[...])

    def hh(r, part):
        return copy(
            yt.at[part, head_rows((head + r) % HEADS_AX)], gh_in.at[part, r - 1],
            h_s.at[part, r - 1], h_r.at[part, r - 1], head_peer(r),
        )

    for c in range(5):
        cols = slice(256 * c, 256 * (c + 1))
        terms = mm(dk_n[:128], wt[width : 2 * width, cols]) + mm(dv_n[:128], wt[2 * width :, cols])
        yt[0, cols, :] = jnp.transpose(terms.astype(BF16))
    for r in range(1, HEADS_AX):
        hh(r, 0).start()
    for r in range(1, CROSS):
        ee(r).wait_recv()
    total = part[cross].astype(F32)
    for r in range(1, CROSS):
        total = total + parts_in[r - 1].astype(F32)

    def piece(k):
        return gw_ref.at[
            pl.ds(pl.multiple_of(win_rows(pos) + 32 * (k // 3), 32), 32),
            pl.ds(pl.multiple_of(win_start(pos) + 128 * (k % 3), 128), 128),
        ]

    def holds(k):
        return (k < 15) & (is_wide(pos) | (k % 3 < 2))

    def ff(r):
        return copy(piece(cross), piece(cross), f_s.at[r - 1], f_r.at[r - 1], cross_peer(r))

    def ff_in(r):
        k = (cross - r + CROSS) % CROSS
        return k, copy(piece(k), piece(k), f_s.at[r - 1], f_r.at[r - 1], cross_peer(r))

    @pl.when(holds(cross))
    def _():
        gw_ref[
            pl.ds(pl.multiple_of(win_rows(pos) + 32 * (cross // 3), 32), 32),
            pl.ds(pl.multiple_of(win_start(pos) + 128 * (cross % 3), 128), 128),
        ] = total.astype(BF16)
        for r in CROSS_FAR_FIRST:
            ff(r).start()

    for c in range(5):
        cols = slice(256 * c, 256 * (c + 1))
        terms = mm(dk_n[128:], wt[width : 2 * width, cols]) + mm(dv_n[128:], wt[2 * width :, cols])
        terms = terms + mm(dq_n, wt[0:width, cols])
        yt[1, cols, :] = jnp.transpose(terms.astype(BF16))
    for r in range(1, HEADS_AX):
        hh(r, 1).start()
    for r in range(1, HEADS_AX):
        hh(r, 0).wait_recv()
    extra = yt[0, head_rows(head), :].astype(F32)
    for r in range(1, HEADS_AX):
        extra = extra + gh_in[0, r - 1].astype(F32)
    pg_lo[...] = pack(extra, 0).astype(BF16)
    pg_hi[...] = pack(extra, 1).astype(BF16)

    def lead_back(p):
        return copy(pg_lo, gin_lo.at[p - 1], z_s.at[0], z_r.at[p - 1], (tm - p, head))

    def prev_back():
        return copy(pg_hi, gin_hi, z_s.at[1], z_r.at[3], (tm - 1, head))

    for p in range(1, SPAN):
        @pl.when(place == p)
        def _(p=p):
            lead_back(p).start()
            prev_back().start()

    for r in range(1, CROSS):
        k, arrival = ff_in(r)

        @pl.when(holds(k))
        def _(arrival=arrival):
            arrival.wait_recv()

    def region(j, tiles, first=0, rows=half_w):
        return gw_ref.at[
            pl.ds(pl.multiple_of(win_rows(j) + first, 16), rows), pl.ds(win_start(j), 128 * tiles)
        ]

    def at(d):
        return (pos + d + GROUP) % GROUP

    def peer_at(d):
        return (tm + (at(d) - pos) * stride, head)

    def hop(slot, j, d, tiles, first=0, rows=half_w):
        ref = region(j, tiles, first, rows)
        return copy(ref, ref, g_s.at[slot], g_r.at[slot], peer_at(d))

    near = ((0, 2), (1, -2), (2, 1), (3, -1))
    onward = (
        (4, -2, 1, 0, half_w), (5, 2, -1, 0, half_w),
        (6, -2, 2, 0, half_w // 2), (7, 2, -2, half_w // 2, half_w // 2),
    )
    for slot, d in near:
        by_tiles(pos, lambda tiles, slot=slot, d=d: hop(slot, pos, d, tiles).start())
    for slot, d in near[:2]:
        by_tiles(at(-d), lambda tiles, slot=slot, d=d: hop(slot, at(-d), d, tiles).wait_recv())
        for out, of, dist, first, rows in onward:
            if of == -d:
                by_tiles(
                    at(of),
                    lambda tiles, out=out, of=of, dist=dist, first=first, rows=rows: hop(
                        out, at(of), dist, tiles, first, rows
                    ).start(),
                )

    for r in range(1, HEADS_AX):
        hh(r, 1).wait_recv()
    own = yt[1, head_rows(head), :].astype(F32)
    for r in range(1, HEADS_AX):
        own = own + gh_in[1, r - 1].astype(F32)

    @pl.when(place == 0)
    def _():
        for p in range(1, SPAN):
            copy(
                pg_lo, gin_lo.at[p - 1], z_s.at[0], z_r.at[p - 1], head_peer(1)
            ).wait_recv()

    @pl.when(place < SPAN - 1)
    def _():
        copy(pg_hi, gin_hi, z_s.at[1], z_r.at[3], head_peer(1)).wait_recv()

    lead_sum = gin_lo[0].astype(F32) + gin_lo[1].astype(F32) + gin_lo[2].astype(F32)
    lead_sum = jnp.where(place == 0, lead_sum, 0.0)
    prev_in = jnp.where(place < SPAN - 1, gin_hi[...].astype(F32), 0.0)
    local = jnp.where((place == 0) & low_lanes(own.shape), extra + roll_half(extra), 0.0)
    gh_ref[...] = (own + local + unpack(lead_sum, prev_in)).astype(BF16)

    for slot, d in near[2:]:
        by_tiles(at(-d), lambda tiles, slot=slot, d=d: hop(slot, at(-d), d, tiles).wait_recv())
    for out, of, dist, first, rows in onward:
        by_tiles(
            at(of - dist),
            lambda tiles, out=out, of=of, dist=dist, first=first, rows=rows: hop(
                out, at(of - dist), dist, tiles, first, rows
            ).wait_recv(),
        )

    for r in range(1, HEADS_AX):
        a1(r).wait_send()
        a3(r).wait_send()
        hh(r, 0).wait_send()
        hh(r, 1).wait_send()

    @pl.when(place == 0)
    def _():
        for p in range(1, SPAN):
            lead_out(p).wait_send()

    @pl.when(place < SPAN - 1)
    def _():
        prev_out().wait_send()

    @pl.when(place > 0)
    def _():
        lead_back(1).wait_send()
        prev_back().wait_send()

    for r in range(1, GROUP):
        by_tiles(group_pos(r), lambda tiles, r=r: fe(r, group_pos(r), tiles).wait_send())
        cc(r).wait_send()
    for slot, d in near:
        by_tiles(pos, lambda tiles, slot=slot, d=d: hop(slot, pos, d, tiles).wait_send())
    for out, of, dist, first, rows in onward:
        by_tiles(
            at(of),
            lambda tiles, out=out, of=of, dist=dist, first=first, rows=rows: hop(
                out, at(of), dist, tiles, first, rows
            ).wait_send(),
        )
    for r in range(1, CROSS):
        ee(r).wait_send()

    @pl.when(holds(cross))
    def _():
        for r in range(1, CROSS):
            ff(r).wait_send()


def hand_out(*refs):
    count = 3
    arrays, outs, held, sem = refs[:count], refs[count : 2 * count], refs[2 * count : -1], refs[-1]
    arrivals = [
        pltpu.make_async_copy(arrays[i], held[i], sem.at[0, i]) for i in range(count)
    ]
    copies = [pltpu.make_async_copy(held[i], outs[i], sem.at[1, i]) for i in range(count)]
    for arrival in arrivals:
        arrival.start()
    for arrival, out in zip(arrivals, copies):
        arrival.wait()
        out.start()
    for out in copies:
        out.wait()


def shards(hidden_states, w_query, w_key, w_value, grad_out):
    rows, width = hidden_states.shape
    full = w_query.shape[0]
    half = width // 2
    vm = pltpu.VMEM
    dma = pltpu.SemaphoreType.DMA
    scratch = [
        vm((full, rows), BF16),
        vm((full, rows), BF16),
        vm((3 * width, full), BF16),
        vm((width, rows), BF16),
        vm((half, 128), BF16), vm((half, 128), BF16),
        vm((half, 128), BF16), vm((half, 128), BF16),
        vm((3 * width, rows), BF16),
        vm((2 * width, rows), BF16),
        vm((2, rows, 2 * width), BF16),
        vm((width, rows), BF16),
        vm((GROUP, WIN, 128), BF16),
        vm((GROUP, half, 128), BF16),
        vm((CROSS, 32, 128), BF16),
        vm((CROSS - 1, 32, 128), BF16),
        vm((2, full, 128), BF16),
        vm((2, HEADS_AX - 1, width, 128), BF16),
        vm((half, 128), BF16), vm((half, 128), BF16),
        vm((SPAN - 1, half, 128), BF16), vm((half, 128), BF16),
        vm((2 * (width // HD), 256, 128), BF16),
        dma((5,)),
        dma((3,)), dma((3,)),
        dma((4,)), dma((2,)),
        dma((3,)), dma((3,)),
        dma((GROUP - 1,)), dma((GROUP - 1,)),
        dma((GROUP - 1,)), dma((GROUP - 1,)),
        dma((CROSS - 1,)), dma((CROSS - 1,)),
        dma((CROSS - 1,)), dma((CROSS - 1,)),
        dma((8,)), dma((8,)),
        dma((2, 3)), dma((2, 3)),
        dma((2,)), dma((4,)),
    ]
    att, gw, gh = pl.pallas_call(
        kernel,
        out_shape=(
            jax.ShapeDtypeStruct((width, rows), BF16),
            jax.ShapeDtypeStruct((width, full), BF16),
            jax.ShapeDtypeStruct((width, rows), BF16),
        ),
        in_specs=[pl.BlockSpec(memory_space=pltpu.HBM)] * 5,
        out_specs=[pl.BlockSpec(memory_space=pltpu.VMEM)] * 3,
        scratch_shapes=scratch,
        compiler_params=pltpu.CompilerParams(
            collective_id=0, has_side_effects=True, vmem_limit_bytes=60 * 2**20
        ),
    )(hidden_states.T, w_query.T, w_key.T, w_value.T, grad_out.T)
    att, gw, gh = pl.pallas_call(
        hand_out,
        out_shape=tuple(jax.ShapeDtypeStruct(a.shape, BF16) for a in (att, gw, gh)),
        in_specs=[pl.BlockSpec(memory_space=pltpu.HBM)] * 3,
        out_specs=[pl.BlockSpec(memory_space=pltpu.HBM)] * 3,
        scratch_shapes=[vm(a.shape, BF16) for a in (att, gw, gh)] + [dma((2, 3))],
        compiler_params=pltpu.CompilerParams(vmem_limit_bytes=60 * 2**20),
    )(att, gw, gh)
    return att.T, gw.T, gh.T


def solution(mesh):
    placed = (P("tm", "head"), P(None, "head"), P(None, "head"), P(None, "head"), P("tm", "head"))
    return jax.shard_map(
        shards,
        mesh=mesh,
        in_specs=placed,
        out_specs=(P("tm", "head"), P(None, "head"), P("tm", "head")),
        check_vma=False,
    )
```

```python
import functools

import jax
import jax.numpy as jnp
from jax import lax
from jax.experimental import pallas as pl
from jax.experimental.pallas import tpu as pltpu
from jax.sharding import PartitionSpec as P

MESH = pl.DeviceIdType.MESH
F32 = jnp.float32
BF16 = jnp.bfloat16

P_SIZE = 64
HD = 64
SPAN = 4
NZ = 8
GROUP = 8
CROSS = 16
HEADS_AX = 4
FAR_FIRST = sorted(range(1, GROUP), key=lambda r: abs(r - GROUP // 2))
CROSS_FAR_FIRST = sorted(range(1, CROSS), key=lambda r: abs(r - CROSS // 2))
WIN = 384
NT = (((1,), (1,)), ((), ()))


def mm(a, b):
    return jnp.dot(a, b, preferred_element_type=F32)


def mm_nt(a, b):
    return lax.dot_general(a, b, NT, preferred_element_type=F32)


def roll_half(x):
    return pltpu.roll(x, P_SIZE, 1)


def low_lanes(shape):
    return lax.broadcasted_iota(jnp.int32, shape, 1) < P_SIZE


def pack(tile, half):
    n = tile.shape[0] // 2
    top, bottom = tile[:n], tile[n:]
    low = low_lanes((n, 128))
    if half == 0:
        return jnp.where(low, top, roll_half(bottom))
    return jnp.where(low, roll_half(top), bottom)


def unpack(first, second):
    low = low_lanes(first.shape)
    return jnp.concatenate(
        [jnp.where(low, first, roll_half(second)), jnp.where(low, roll_half(first), second)], 0
    )


def kernel(
    hid_ref, wq_ref, wk_ref, wv_ref, go_ref,
    att_ref, gw_ref, gh_ref,
    xt, et, wt, gt, pk_lo, pk_hi, in_lo, in_hi,
    qkv, kve, kvn, dqt, fall, dqall, part, parts_in, yt, gh_in, pg_lo, pg_hi, gin_lo, gin_hi,
    pts, local_sem, a1_s, a1_r, a2_s, a2_r, a3_s, a3_r, fe_s, fe_r, c_s, c_r,
    e_s, e_r, f_s, f_r, g_s, g_r, h_s, h_r, z_s, z_r,
):
    tm = lax.axis_index("tm")
    head = lax.axis_index("head")
    core = head % 2
    z = tm % NZ
    xh = (tm // NZ) % 2
    y = tm // (2 * NZ)
    place = z % SPAN
    pos = (1 - core) * z + core * y
    stride = (1 - core) + core * 2 * NZ
    pos2 = (1 - core) * y + core * z
    stride2 = (1 - core) * 2 * NZ + core
    cross = pos2 * 2 + xh
    width = hid_ref.shape[0]
    half_w = width // 2

    def copy(src, dst, send, recv, device):
        return pltpu.make_async_remote_copy(
            src_ref=src, dst_ref=dst, send_sem=send, recv_sem=recv,
            device_id=device, device_id_type=MESH,
        )

    def head_peer(r):
        return (tm, (head + r) % HEADS_AX)

    def group_pos(r):
        return (pos + r) % GROUP

    def group_peer(r):
        return (tm + (group_pos(r) - pos) * stride, head)

    def cross_pos(r):
        return (cross + r) % CROSS

    def cross_peer(r):
        k = cross_pos(r)
        return (tm + (k // 2 - pos2) * stride2 + (k % 2 - xh) * NZ, head)

    def head_rows(h):
        return pl.ds(pl.multiple_of(h * width, 64), width)

    def is_wide(j):
        return (j // 2) % 2 == 0

    def by_tiles(j, run):
        pl.when(is_wide(j))(lambda: run(3))
        pl.when(jnp.logical_not(is_wide(j)))(lambda: run(2))

    def win_start(j):
        a = j // 2
        return pl.multiple_of(640 * (a // 2) + 384 * (a % 2), 128)

    def win_rows(j):
        return pl.multiple_of((j % 2) * half_w, 32)

    barrier = pltpu.get_barrier_semaphore()
    peers = (
        [head_peer(r) for r in range(1, HEADS_AX)]
        + [group_peer(r) for r in range(1, GROUP)]
        + [cross_peer(r) for r in range(1, CROSS)]
    )
    for peer in peers:
        pl.semaphore_signal(barrier, inc=1, device_id=peer, device_id_type=MESH)

    own_x = xt.at[head_rows(head)]
    loads = [
        pltpu.make_async_copy(hid_ref, own_x, local_sem.at[0]),
        pltpu.make_async_copy(wq_ref, wt.at[pl.ds(0, width)], local_sem.at[1]),
        pltpu.make_async_copy(wk_ref, wt.at[pl.ds(width, width)], local_sem.at[2]),
        pltpu.make_async_copy(wv_ref, wt.at[pl.ds(2 * width, width)], local_sem.at[3]),
        pltpu.make_async_copy(go_ref, gt, local_sem.at[4]),
    ]
    for load in loads:
        load.start()
    loads[0].wait()
    tile = xt[head_rows(head), :].astype(F32)
    pk_lo[...] = pack(tile, 0).astype(BF16)
    pk_hi[...] = pack(tile, 1).astype(BF16)
    pl.semaphore_wait(barrier, len(peers))

    def a1(r):
        return copy(own_x, own_x, a1_s.at[r - 1], a1_r.at[r - 1], head_peer(r))

    def a1_in(r):
        rows = xt.at[head_rows((head - r + HEADS_AX) % HEADS_AX)]
        return copy(rows, rows, a1_s.at[r - 1], a1_r.at[r - 1], head_peer(r))

    for r in range(1, HEADS_AX):
        a1(r).start()

    def lead_out(p):
        return copy(pk_lo, in_lo, a2_s.at[p - 1], a2_r.at[0], (tm + p, head))

    def prev_out():
        return copy(pk_hi, in_hi, a2_s.at[3], a2_r.at[1], (tm + 1, head))

    @pl.when(place == 0)
    def _():
        for p in reversed(range(1, SPAN)):
            lead_out(p).start()

    @pl.when(place < SPAN - 1)
    def _():
        prev_out().start()

    own_e = et.at[head_rows(head)]

    @pl.when(place == 0)
    def _():
        et[head_rows(head), :] = jnp.where(low_lanes(tile.shape), tile, roll_half(tile)).astype(BF16)

    @pl.when(place > 0)
    def _():
        copy(pk_lo, in_lo, a2_s.at[0], a2_r.at[0], (tm, (head + 1) % HEADS_AX)).wait_recv()
        copy(pk_hi, in_hi, a2_s.at[3], a2_r.at[1], (tm, (head + 1) % HEADS_AX)).wait_recv()
        et[head_rows(head), :] = unpack(in_lo[...].astype(F32), in_hi[...].astype(F32)).astype(BF16)

    def a3(r):
        return copy(own_e, own_e, a3_s.at[r - 1], a3_r.at[r - 1], head_peer(r))

    def a3_in(r):
        rows = et.at[head_rows((head - r + HEADS_AX) % HEADS_AX)]
        return copy(rows, rows, a3_s.at[r - 1], a3_r.at[r - 1], head_peer(r))

    for r in range(1, HEADS_AX):
        a3(r).start()
    for r in range(1, HEADS_AX):
        a1_in(r).wait_recv()

    def fe(r, j, tiles):
        return copy(
            xt.at[pl.ds(win_start(j), 128 * tiles)], fall.at[r, pl.ds(0, 128 * tiles)],
            fe_s.at[r - 1], fe_r.at[r - 1], group_peer(r),
        )

    for r in FAR_FIRST:
        by_tiles(group_pos(r), lambda tiles, r=r: fe(r, group_pos(r), tiles).start())

    @pl.when(is_wide(pos))
    def _():
        fall[0] = xt[pl.ds(win_start(pos), 384), :]

    @pl.when(jnp.logical_not(is_wide(pos)))
    def _():
        fall[0, 0:256] = xt[pl.ds(win_start(pos), 256), :]
        for r in range(GROUP):
            fall[r, 256:384] = jnp.zeros((128, 128), BF16)

    for load in loads[1:]:
        load.wait()
    qkv[...] = mm(wt[...], xt[...]).astype(BF16)
    kvn[1] = jnp.transpose(qkv[width:, :])
    for r in range(1, HEADS_AX):
        a3_in(r).wait_recv()
    kve[...] = mm(wt[width:, :], et[...]).astype(BF16)
    kvn[0] = jnp.transpose(kve[...])

    scale = HD ** (-0.5)
    low = low_lanes((P_SIZE, 128))
    zero = jnp.zeros((P_SIZE, 128), BF16)
    heads_here = width // HD

    def spread(lead, second, index):
        pts[index, 0:64, :] = lead
        pts[index, 64:128, :] = jnp.where(low, second, zero)
        pts[index, 128:192, :] = jnp.where(low, zero, second)
        pts[index, 192:256, :] = zero

    def cc(r):
        return copy(
            dqt.at[pl.ds(win_rows(group_pos(r)), half_w)], dqall.at[r],
            c_s.at[r - 1], c_r.at[r - 1], group_peer(r),
        )

    def send_half(part):
        for r in FAR_FIRST:
            pl.when(group_pos(r) % 2 == part)(lambda r=r: cc(r).start())

    for i in range(heads_here):
        a, b = HD * i, HD * (i + 1)
        q = qkv[a:b, :]
        cot = gt[a:b, :]
        k_extra, k_own = kvn[0, :, a:b], kvn[1, 0:64, a:b]
        v_extra, v_own = kvn[0, :, width + a : width + b], kvn[1, 0:64, width + a : width + b]
        s_extra, s_own = mm(k_extra, q) * scale, mm(k_own, q) * scale
        s_lead, s_second = s_extra[:64], jnp.where(low, s_extra[64:], s_own)
        top = jnp.maximum(
            jnp.max(s_lead, 0, keepdims=True), jnp.max(s_second, 0, keepdims=True)
        )
        e_lead, e_second = jnp.exp(s_lead - top), jnp.exp(s_second - top)
        inv = 1.0 / (jnp.sum(e_lead, 0, keepdims=True) + jnp.sum(e_second, 0, keepdims=True))
        p_lead, p_second = e_lead * inv, e_second * inv
        d_extra, d_own = mm(v_extra, cot), mm(v_own, cot)
        d_lead, d_second = d_extra[:64], jnp.where(low, d_extra[64:], d_own)
        inner = jnp.sum(p_lead * d_lead, 0, keepdims=True) + jnp.sum(
            p_second * d_second, 0, keepdims=True
        )
        spread(
            (p_lead * (d_lead - inner) * scale).astype(BF16),
            (p_second * (d_second - inner) * scale).astype(BF16),
            2 * i,
        )
        spread(p_lead.astype(BF16), p_second.astype(BF16), 2 * i + 1)
        k_wide = jnp.concatenate([kve[a:b, :], qkv[width + a : width + b, :]], 1)
        dqt[a:b, :] = mm(k_wide, pts[2 * i]).astype(BF16)
        if a < half_w <= b:
            send_half(0)
    send_half(1)
    dqall[0] = dqt[pl.ds(win_rows(pos), half_w), :]


    dks, dvs = [], []
    for i in range(heads_here):
        a, b = HD * i, HD * (i + 1)
        v_wide = jnp.concatenate(
            [kve[width + a : width + b, :], qkv[2 * width + a : 2 * width + b, :]], 1
        )
        att_ref[a:b, :] = mm(v_wide, pts[2 * i + 1]).astype(BF16)
        dks.append(mm_nt(qkv[a:b, :], pts[2 * i]).astype(BF16))
        dvs.append(mm_nt(gt[a:b, :], pts[2 * i + 1]).astype(BF16))

    for r in range(1, GROUP):
        by_tiles(pos, lambda tiles, r=r: fe(r, pos, tiles).wait_recv())
    near_blocks, far_blocks = (0, 1, 7, 2), (6, 3, 5, 4)

    def products(blocks):
        for r in blocks:
            if r:
                cc(r).wait_recv()
        return mm_nt(
            jnp.concatenate([dqall[r] for r in blocks], 1),
            jnp.concatenate([fall[r] for r in blocks], 1),
        )

    window = products(near_blocks)
    window = (window + products(far_blocks)).astype(BF16)
    for k in range(15):
        i, l = k // 3, k % 3
        part[k] = window[32 * i : 32 * i + 32, 128 * l : 128 * l + 128]

    def holds(k):
        return (k < 15) & (is_wide(pos) | (k % 3 < 2))

    def ee(r):
        return copy(
            part.at[cross_pos(r)], parts_in.at[r - 1], e_s.at[r - 1], e_r.at[r - 1], cross_peer(r)
        )

    for r in CROSS_FAR_FIRST:
        pl.when(holds(cross_pos(r)))(lambda r=r: ee(r).start())

    dk_n = jnp.transpose(jnp.concatenate(dks, 0))
    dv_n = jnp.transpose(jnp.concatenate(dvs, 0))
    dq_n = jnp.transpose(dqt[...])

    def hh(r, part):
        return copy(
            yt.at[part, head_rows((head + r) % HEADS_AX)], gh_in.at[part, r - 1],
            h_s.at[part, r - 1], h_r.at[part, r - 1], head_peer(r),
        )

    for c in range(5):
        cols = slice(256 * c, 256 * (c + 1))
        terms = mm(dk_n[:128], wt[width : 2 * width, cols]) + mm(dv_n[:128], wt[2 * width :, cols])
        yt[0, cols, :] = jnp.transpose(terms.astype(BF16))
    for r in range(1, HEADS_AX):
        hh(r, 0).start()

    def piece(k):
        return gw_ref.at[
            pl.ds(pl.multiple_of(win_rows(pos) + 32 * (k // 3), 32), 32),
            pl.ds(pl.multiple_of(win_start(pos) + 128 * (k % 3), 128), 128),
        ]

    def ff(r):
        return copy(piece(cross), piece(cross), f_s.at[r - 1], f_r.at[r - 1], cross_peer(r))

    def ff_in(r):
        k = (cross - r + CROSS) % CROSS
        return k, copy(piece(k), piece(k), f_s.at[r - 1], f_r.at[r - 1], cross_peer(r))

    @pl.when(holds(cross))
    def _():
        total = part[cross].astype(F32)
        for r in reversed(CROSS_FAR_FIRST):
            ee(r).wait_recv()
            total = total + parts_in[r - 1].astype(F32)
        gw_ref[
            pl.ds(pl.multiple_of(win_rows(pos) + 32 * (cross // 3), 32), 32),
            pl.ds(pl.multiple_of(win_start(pos) + 128 * (cross % 3), 128), 128),
        ] = total.astype(BF16)
        for r in CROSS_FAR_FIRST:
            ff(r).start()

    for c in range(5):
        cols = slice(256 * c, 256 * (c + 1))
        terms = mm(dk_n[128:], wt[width : 2 * width, cols]) + mm(dv_n[128:], wt[2 * width :, cols])
        terms = terms + mm(dq_n, wt[0:width, cols])
        yt[1, cols, :] = jnp.transpose(terms.astype(BF16))

    for r in range(1, HEADS_AX):
        hh(r, 1).start()
    for r in range(1, HEADS_AX):
        hh(r, 0).wait_recv()
    extra = yt[0, head_rows(head), :].astype(F32)
    for r in range(1, HEADS_AX):
        extra = extra + gh_in[0, r - 1].astype(F32)
    pg_lo[...] = pack(extra, 0).astype(BF16)
    pg_hi[...] = pack(extra, 1).astype(BF16)

    def lead_back(p):
        return copy(pg_lo, gin_lo.at[p - 1], z_s.at[0], z_r.at[p - 1], (tm - p, head))

    def prev_back():
        return copy(pg_hi, gin_hi, z_s.at[1], z_r.at[3], (tm - 1, head))

    for p in range(1, SPAN):
        @pl.when(place == p)
        def _(p=p):
            lead_back(p).start()
            prev_back().start()

    for r in range(1, CROSS):
        k, arrival = ff_in(r)

        @pl.when(holds(k))
        def _(arrival=arrival):
            arrival.wait_recv()

    def region(j, tiles, first=0, rows=half_w):
        return gw_ref.at[
            pl.ds(pl.multiple_of(win_rows(j) + first, 16), rows), pl.ds(win_start(j), 128 * tiles)
        ]

    def at(d):
        return (pos + d + GROUP) % GROUP

    def peer_at(d):
        return (tm + (at(d) - pos) * stride, head)

    def hop(slot, j, d, tiles, first=0, rows=half_w):
        ref = region(j, tiles, first, rows)
        return copy(ref, ref, g_s.at[slot], g_r.at[slot], peer_at(d))

    half_r = half_w // 2
    near = (
        (0, 2, 0, half_r), (1, -2, half_r, half_r), (2, 2, half_r, half_r), (3, -2, 0, half_r),
        (4, 1, 0, half_w), (5, -1, 0, half_w),
    )
    onward = {
        0: ((6, -2, 2, 0, half_r), (7, -2, 1, 0, half_r)),
        1: ((8, 2, -2, half_r, half_r), (9, 2, -1, half_r, half_r)),
        2: ((10, -2, 1, half_r, half_r),),
        3: ((11, 2, -1, 0, half_r),),
    }

    def start(slot, j, *how):
        by_tiles(j, lambda tiles: hop(slot, j, how[0], tiles, *how[1:]).start())

    def arrived(slot, j, *how):
        by_tiles(j, lambda tiles: hop(slot, j, how[0], tiles, *how[1:]).wait_recv())

    def left(slot, j, *how):
        by_tiles(j, lambda tiles: hop(slot, j, how[0], tiles, *how[1:]).wait_send())

    for slot, *how in near:
        start(slot, pos, *how)
    for slot, d, *rows in near[:4]:
        arrived(slot, at(-d), d, *rows)
        for out, of, *how in onward[slot]:
            start(out, at(of), *how)

    for r in range(1, HEADS_AX):
        hh(r, 1).wait_recv()
    own = yt[1, head_rows(head), :].astype(F32)
    for r in range(1, HEADS_AX):
        own = own + gh_in[1, r - 1].astype(F32)

    @pl.when(place == 0)
    def _():
        for p in range(1, SPAN):
            copy(
                pg_lo, gin_lo.at[p - 1], z_s.at[0], z_r.at[p - 1], head_peer(1)
            ).wait_recv()

    @pl.when(place < SPAN - 1)
    def _():
        copy(pg_hi, gin_hi, z_s.at[1], z_r.at[3], head_peer(1)).wait_recv()

    lead_sum = gin_lo[0].astype(F32) + gin_lo[1].astype(F32) + gin_lo[2].astype(F32)
    lead_sum = jnp.where(place == 0, lead_sum, 0.0)
    prev_in = jnp.where(place < SPAN - 1, gin_hi[...].astype(F32), 0.0)
    local = jnp.where((place == 0) & low_lanes(own.shape), extra + roll_half(extra), 0.0)
    gh_ref[...] = (own + local + unpack(lead_sum, prev_in)).astype(BF16)

    for slot, d, *rows in near[4:]:
        arrived(slot, at(-d), d, *rows)
    for sends in onward.values():
        for out, of, dist, *rows in sends:
            arrived(out, at(of - dist), dist, *rows)

    for r in range(1, HEADS_AX):
        a1(r).wait_send()
        a3(r).wait_send()
        hh(r, 0).wait_send()
        hh(r, 1).wait_send()

    @pl.when(place == 0)
    def _():
        for p in range(1, SPAN):
            lead_out(p).wait_send()

    @pl.when(place < SPAN - 1)
    def _():
        prev_out().wait_send()

    @pl.when(place > 0)
    def _():
        lead_back(1).wait_send()
        prev_back().wait_send()

    for r in range(1, GROUP):
        by_tiles(group_pos(r), lambda tiles, r=r: fe(r, group_pos(r), tiles).wait_send())
        cc(r).wait_send()
    for slot, *how in near:
        left(slot, pos, *how)
    for sends in onward.values():
        for out, of, *how in sends:
            left(out, at(of), *how)
    for r in range(1, CROSS):
        pl.when(holds(cross_pos(r)))(lambda r=r: ee(r).wait_send())

    @pl.when(holds(cross))
    def _():
        for r in range(1, CROSS):
            ff(r).wait_send()


def hand_out(*refs):
    count = 3
    arrays, outs, held, sem = refs[:count], refs[count : 2 * count], refs[2 * count : -1], refs[-1]
    arrivals = [
        pltpu.make_async_copy(arrays[i], held[i], sem.at[0, i]) for i in range(count)
    ]
    copies = [pltpu.make_async_copy(held[i], outs[i], sem.at[1, i]) for i in range(count)]
    for arrival in arrivals:
        arrival.start()
    for arrival, out in zip(arrivals, copies):
        arrival.wait()
        out.start()
    for out in copies:
        out.wait()


def shards(hidden_states, w_query, w_key, w_value, grad_out):
    rows, width = hidden_states.shape
    full = w_query.shape[0]
    half = width // 2
    vm = pltpu.VMEM
    dma = pltpu.SemaphoreType.DMA
    scratch = [
        vm((full, rows), BF16),
        vm((full, rows), BF16),
        vm((3 * width, full), BF16),
        vm((width, rows), BF16),
        vm((half, 128), BF16), vm((half, 128), BF16),
        vm((half, 128), BF16), vm((half, 128), BF16),
        vm((3 * width, rows), BF16),
        vm((2 * width, rows), BF16),
        vm((2, rows, 2 * width), BF16),
        vm((width, rows), BF16),
        vm((GROUP, WIN, 128), BF16),
        vm((GROUP, half, 128), BF16),
        vm((CROSS, 32, 128), BF16),
        vm((CROSS - 1, 32, 128), BF16),
        vm((2, full, 128), BF16),
        vm((2, HEADS_AX - 1, width, 128), BF16),
        vm((half, 128), BF16), vm((half, 128), BF16),
        vm((SPAN - 1, half, 128), BF16), vm((half, 128), BF16),
        vm((2 * (width // HD), 256, 128), BF16),
        dma((5,)),
        dma((3,)), dma((3,)),
        dma((4,)), dma((2,)),
        dma((3,)), dma((3,)),
        dma((GROUP - 1,)), dma((GROUP - 1,)),
        dma((GROUP - 1,)), dma((GROUP - 1,)),
        dma((CROSS - 1,)), dma((CROSS - 1,)),
        dma((CROSS - 1,)), dma((CROSS - 1,)),
        dma((12,)), dma((12,)),
        dma((2, 3)), dma((2, 3)),
        dma((2,)), dma((4,)),
    ]
    att, gw, gh = pl.pallas_call(
        kernel,
        out_shape=(
            jax.ShapeDtypeStruct((width, rows), BF16),
            jax.ShapeDtypeStruct((width, full), BF16),
            jax.ShapeDtypeStruct((width, rows), BF16),
        ),
        in_specs=[pl.BlockSpec(memory_space=pltpu.HBM)] * 5,
        out_specs=[pl.BlockSpec(memory_space=pltpu.VMEM)] * 3,
        scratch_shapes=scratch,
        compiler_params=pltpu.CompilerParams(
            collective_id=0, has_side_effects=True, vmem_limit_bytes=60 * 2**20
        ),
    )(hidden_states.T, w_query.T, w_key.T, w_value.T, grad_out.T)
    att, gw, gh = pl.pallas_call(
        hand_out,
        out_shape=tuple(jax.ShapeDtypeStruct(a.shape, BF16) for a in (att, gw, gh)),
        in_specs=[pl.BlockSpec(memory_space=pltpu.HBM)] * 3,
        out_specs=[pl.BlockSpec(memory_space=pltpu.HBM)] * 3,
        scratch_shapes=[vm(a.shape, BF16) for a in (att, gw, gh)] + [dma((2, 3))],
        compiler_params=pltpu.CompilerParams(vmem_limit_bytes=60 * 2**20),
    )(att, gw, gh)
    return att.T, gw.T, gh.T


def solution(mesh):
    placed = (P("tm", "head"), P(None, "head"), P(None, "head"), P(None, "head"), P("tm", "head"))
    return jax.shard_map(
        shards,
        mesh=mesh,
        in_specs=placed,
        out_specs=(P("tm", "head"), P(None, "head"), P("tm", "head")),
        check_vma=False,
    )
```

```python
import functools

import jax
import jax.numpy as jnp
from jax import lax
from jax.experimental import pallas as pl
from jax.experimental.pallas import tpu as pltpu
from jax.sharding import PartitionSpec as P

MESH = pl.DeviceIdType.MESH
F32 = jnp.float32
BF16 = jnp.bfloat16

P_SIZE = 64
HD = 64
SPAN = 4
NZ = 8
GROUP = 8
CROSS = 16
HEADS_AX = 4
FAR_FIRST = sorted(range(1, GROUP), key=lambda r: abs(r - GROUP // 2))
CROSS_FAR_FIRST = sorted(range(1, CROSS), key=lambda r: abs(r - CROSS // 2))
WIN = 384
NT = (((1,), (1,)), ((), ()))


def mm(a, b):
    return jnp.dot(a, b, preferred_element_type=F32)


def mm_nt(a, b):
    return lax.dot_general(a, b, NT, preferred_element_type=F32)


def roll_half(x):
    return pltpu.roll(x, P_SIZE, 1)


def low_lanes(shape):
    return lax.broadcasted_iota(jnp.int32, shape, 1) < P_SIZE


def pack(tile, half):
    n = tile.shape[0] // 2
    top, bottom = tile[:n], tile[n:]
    low = low_lanes((n, 128))
    if half == 0:
        return jnp.where(low, top, roll_half(bottom))
    return jnp.where(low, roll_half(top), bottom)


def unpack(first, second):
    low = low_lanes(first.shape)
    return jnp.concatenate(
        [jnp.where(low, first, roll_half(second)), jnp.where(low, roll_half(first), second)], 0
    )


def kernel(
    hid_ref, wq_ref, wk_ref, wv_ref, go_ref,
    att_ref, gw_ref, gh_ref,
    xt, et, wt, gt, pk_lo, pk_hi, in_lo, in_hi,
    qkv, kve, kvn, dqt, fall, dqall, part, parts_in, yt, gh_in, pg_lo, pg_hi, gin_lo, gin_hi,
    pts, local_sem, a1_s, a1_r, a2_s, a2_r, a3_s, a3_r, fe_s, fe_r, c_s, c_r,
    e_s, e_r, f_s, f_r, g_s, g_r, h_s, h_r, z_s, z_r,
):
    tm = lax.axis_index("tm")
    head = lax.axis_index("head")
    core = head % 2
    z = tm % NZ
    xh = (tm // NZ) % 2
    y = tm // (2 * NZ)
    place = z % SPAN
    pos = (1 - core) * z + core * y
    stride = (1 - core) + core * 2 * NZ
    pos2 = (1 - core) * y + core * z
    stride2 = (1 - core) * 2 * NZ + core
    cross = pos2 * 2 + xh
    width = hid_ref.shape[0]
    half_w = width // 2

    def copy(src, dst, send, recv, device):
        return pltpu.make_async_remote_copy(
            src_ref=src, dst_ref=dst, send_sem=send, recv_sem=recv,
            device_id=device, device_id_type=MESH,
        )

    def head_peer(r):
        return (tm, (head + r) % HEADS_AX)

    def group_pos(r):
        return (pos + r) % GROUP

    def group_peer(r):
        return (tm + (group_pos(r) - pos) * stride, head)

    def cross_pos(r):
        return (cross + r) % CROSS

    def cross_peer(r):
        k = cross_pos(r)
        return (tm + (k // 2 - pos2) * stride2 + (k % 2 - xh) * NZ, head)

    def head_rows(h):
        return pl.ds(pl.multiple_of(h * width, 64), width)

    def is_wide(j):
        return (j // 2) % 2 == 0

    def by_tiles(j, run):
        pl.when(is_wide(j))(lambda: run(3))
        pl.when(jnp.logical_not(is_wide(j)))(lambda: run(2))

    def win_start(j):
        a = j // 2
        return pl.multiple_of(640 * (a // 2) + 384 * (a % 2), 128)

    def win_rows(j):
        return pl.multiple_of((j % 2) * half_w, 32)

    barrier = pltpu.get_barrier_semaphore()
    peers = (
        [head_peer(r) for r in range(1, HEADS_AX)]
        + [group_peer(r) for r in range(1, GROUP)]
        + [cross_peer(r) for r in range(1, CROSS)]
    )
    for peer in peers:
        pl.semaphore_signal(barrier, inc=1, device_id=peer, device_id_type=MESH)

    own_x = xt.at[head_rows(head)]
    loads = [
        pltpu.make_async_copy(hid_ref, own_x, local_sem.at[0]),
        pltpu.make_async_copy(wq_ref, wt.at[pl.ds(0, width)], local_sem.at[1]),
        pltpu.make_async_copy(wk_ref, wt.at[pl.ds(width, width)], local_sem.at[2]),
        pltpu.make_async_copy(wv_ref, wt.at[pl.ds(2 * width, width)], local_sem.at[3]),
        pltpu.make_async_copy(go_ref, gt, local_sem.at[4]),
    ]
    for load in loads:
        load.start()
    loads[0].wait()
    tile = xt[head_rows(head), :].astype(F32)
    pk_lo[...] = pack(tile, 0).astype(BF16)
    pk_hi[...] = pack(tile, 1).astype(BF16)
    pl.semaphore_wait(barrier, len(peers))

    def a1(r):
        return copy(own_x, own_x, a1_s.at[r - 1], a1_r.at[r - 1], head_peer(r))

    def a1_in(r):
        rows = xt.at[head_rows((head - r + HEADS_AX) % HEADS_AX)]
        return copy(rows, rows, a1_s.at[r - 1], a1_r.at[r - 1], head_peer(r))

    for r in range(1, HEADS_AX):
        a1(r).start()

    def lead_out(p):
        return copy(pk_lo, in_lo, a2_s.at[p - 1], a2_r.at[0], (tm + p, head))

    def prev_out():
        return copy(pk_hi, in_hi, a2_s.at[3], a2_r.at[1], (tm + 1, head))

    @pl.when(place == 0)
    def _():
        for p in reversed(range(1, SPAN)):
            lead_out(p).start()

    @pl.when(place < SPAN - 1)
    def _():
        prev_out().start()

    own_e = et.at[head_rows(head)]

    @pl.when(place == 0)
    def _():
        et[head_rows(head), :] = jnp.where(low_lanes(tile.shape), tile, roll_half(tile)).astype(BF16)

    @pl.when(place > 0)
    def _():
        copy(pk_lo, in_lo, a2_s.at[0], a2_r.at[0], (tm, (head + 1) % HEADS_AX)).wait_recv()
        copy(pk_hi, in_hi, a2_s.at[3], a2_r.at[1], (tm, (head + 1) % HEADS_AX)).wait_recv()
        et[head_rows(head), :] = unpack(in_lo[...].astype(F32), in_hi[...].astype(F32)).astype(BF16)

    def a3(r):
        return copy(own_e, own_e, a3_s.at[r - 1], a3_r.at[r - 1], head_peer(r))

    def a3_in(r):
        rows = et.at[head_rows((head - r + HEADS_AX) % HEADS_AX)]
        return copy(rows, rows, a3_s.at[r - 1], a3_r.at[r - 1], head_peer(r))

    for r in range(1, HEADS_AX):
        a3(r).start()
    for r in range(1, HEADS_AX):
        a1_in(r).wait_recv()

    def fe(r, j, tiles):
        return copy(
            xt.at[pl.ds(win_start(j), 128 * tiles)], fall.at[r, pl.ds(0, 128 * tiles)],
            fe_s.at[r - 1], fe_r.at[r - 1], group_peer(r),
        )

    for r in FAR_FIRST:
        by_tiles(group_pos(r), lambda tiles, r=r: fe(r, group_pos(r), tiles).start())

    @pl.when(is_wide(pos))
    def _():
        fall[0] = xt[pl.ds(win_start(pos), 384), :]

    @pl.when(jnp.logical_not(is_wide(pos)))
    def _():
        fall[0, 0:256] = xt[pl.ds(win_start(pos), 256), :]
        for r in range(GROUP):
            fall[r, 256:384] = jnp.zeros((128, 128), BF16)

    for load in loads[1:]:
        load.wait()
    qkv[...] = mm(wt[...], xt[...]).astype(BF16)
    kvn[1] = jnp.transpose(qkv[width:, :])
    for r in range(1, HEADS_AX):
        a3_in(r).wait_recv()
    kve[...] = mm(wt[width:, :], et[...]).astype(BF16)
    kvn[0] = jnp.transpose(kve[...])

    scale = HD ** (-0.5)
    low = low_lanes((P_SIZE, 128))
    zero = jnp.zeros((P_SIZE, 128), BF16)
    heads_here = width // HD

    def spread(lead, second, index):
        pts[index, 0:64, :] = lead
        pts[index, 64:128, :] = jnp.where(low, second, zero)
        pts[index, 128:192, :] = jnp.where(low, zero, second)
        pts[index, 192:256, :] = zero

    def cc(r):
        return copy(
            dqt.at[pl.ds(win_rows(group_pos(r)), half_w)], dqall.at[r],
            c_s.at[r - 1], c_r.at[r - 1], group_peer(r),
        )

    for i in range(heads_here):
        a, b = HD * i, HD * (i + 1)
        q = qkv[a:b, :]
        cot = gt[a:b, :]
        k_extra, k_own = kvn[0, :, a:b], kvn[1, 0:64, a:b]
        v_extra, v_own = kvn[0, :, width + a : width + b], kvn[1, 0:64, width + a : width + b]
        s_extra, s_own = mm(k_extra, q) * scale, mm(k_own, q) * scale
        s_lead, s_second = s_extra[:64], jnp.where(low, s_extra[64:], s_own)
        top = jnp.maximum(
            jnp.max(s_lead, 0, keepdims=True), jnp.max(s_second, 0, keepdims=True)
        )
        e_lead, e_second = jnp.exp(s_lead - top), jnp.exp(s_second - top)
        inv = 1.0 / (jnp.sum(e_lead, 0, keepdims=True) + jnp.sum(e_second, 0, keepdims=True))
        p_lead, p_second = e_lead * inv, e_second * inv
        d_extra, d_own = mm(v_extra, cot), mm(v_own, cot)
        d_lead, d_second = d_extra[:64], jnp.where(low, d_extra[64:], d_own)
        inner = jnp.sum(p_lead * d_lead, 0, keepdims=True) + jnp.sum(
            p_second * d_second, 0, keepdims=True
        )
        spread(
            (p_lead * (d_lead - inner) * scale).astype(BF16),
            (p_second * (d_second - inner) * scale).astype(BF16),
            2 * i,
        )
        spread(p_lead.astype(BF16), p_second.astype(BF16), 2 * i + 1)
        k_wide = jnp.concatenate([kve[a:b, :], qkv[width + a : width + b, :]], 1)
        dqt[a:b, :] = mm(k_wide, pts[2 * i]).astype(BF16)
    for r in FAR_FIRST:
        cc(r).start()
    dqall[0] = dqt[pl.ds(win_rows(pos), half_w), :]


    dks, dvs = [], []
    for i in range(heads_here):
        a, b = HD * i, HD * (i + 1)
        v_wide = jnp.concatenate(
            [kve[width + a : width + b, :], qkv[2 * width + a : 2 * width + b, :]], 1
        )
        att_ref[a:b, :] = mm(v_wide, pts[2 * i + 1]).astype(BF16)
        dks.append(mm_nt(qkv[a:b, :], pts[2 * i]).astype(BF16))
        dvs.append(mm_nt(gt[a:b, :], pts[2 * i + 1]).astype(BF16))

    for r in range(1, GROUP):
        by_tiles(pos, lambda tiles, r=r: fe(r, pos, tiles).wait_recv())
    near_blocks, far_blocks = (0, 1, 7, 2), (6, 3, 5, 4)

    def products(blocks):
        for r in blocks:
            if r:
                cc(r).wait_recv()
        return mm_nt(
            jnp.concatenate([dqall[r] for r in blocks], 1),
            jnp.concatenate([fall[r] for r in blocks], 1),
        )

    window = products(near_blocks)
    window = (window + products(far_blocks)).astype(BF16)
    for k in range(15):
        i, l = k // 3, k % 3
        part[k] = window[32 * i : 32 * i + 32, 128 * l : 128 * l + 128]

    def holds(k):
        return (k < 15) & (is_wide(pos) | (k % 3 < 2))

    def ee(r):
        return copy(
            part.at[cross_pos(r)], parts_in.at[r - 1], e_s.at[r - 1], e_r.at[r - 1], cross_peer(r)
        )

    for r in CROSS_FAR_FIRST:
        pl.when(holds(cross_pos(r)))(lambda r=r: ee(r).start())

    dk_n = jnp.transpose(jnp.concatenate(dks, 0))
    dv_n = jnp.transpose(jnp.concatenate(dvs, 0))
    dq_n = jnp.transpose(dqt[...])

    def hh(r, part):
        return copy(
            yt.at[part, head_rows((head + r) % HEADS_AX)], gh_in.at[part, r - 1],
            h_s.at[part, r - 1], h_r.at[part, r - 1], head_peer(r),
        )

    for c in range(5):
        cols = slice(256 * c, 256 * (c + 1))
        terms = mm(dk_n[:128], wt[width : 2 * width, cols]) + mm(dv_n[:128], wt[2 * width :, cols])
        yt[0, cols, :] = jnp.transpose(terms.astype(BF16))
    for r in range(1, HEADS_AX):
        hh(r, 0).start()

    def piece(k):
        return gw_ref.at[
            pl.ds(pl.multiple_of(win_rows(pos) + 32 * (k // 3), 32), 32),
            pl.ds(pl.multiple_of(win_start(pos) + 128 * (k % 3), 128), 128),
        ]

    def ff(r):
        return copy(piece(cross), piece(cross), f_s.at[r - 1], f_r.at[r - 1], cross_peer(r))

    def ff_in(r):
        k = (cross - r + CROSS) % CROSS
        return k, copy(piece(k), piece(k), f_s.at[r - 1], f_r.at[r - 1], cross_peer(r))

    @pl.when(holds(cross))
    def _():
        total = part[cross].astype(F32)
        for r in reversed(CROSS_FAR_FIRST):
            ee(r).wait_recv()
            total = total + parts_in[r - 1].astype(F32)
        gw_ref[
            pl.ds(pl.multiple_of(win_rows(pos) + 32 * (cross // 3), 32), 32),
            pl.ds(pl.multiple_of(win_start(pos) + 128 * (cross % 3), 128), 128),
        ] = total.astype(BF16)
        for r in CROSS_FAR_FIRST:
            ff(r).start()

    for c in range(5):
        cols = slice(256 * c, 256 * (c + 1))
        terms = mm(dk_n[128:], wt[width : 2 * width, cols]) + mm(dv_n[128:], wt[2 * width :, cols])
        terms = terms + mm(dq_n, wt[0:width, cols])
        yt[1, cols, :] = jnp.transpose(terms.astype(BF16))

    for r in range(1, HEADS_AX):
        hh(r, 1).start()
    for r in range(1, HEADS_AX):
        hh(r, 0).wait_recv()
    extra = yt[0, head_rows(head), :].astype(F32)
    for r in range(1, HEADS_AX):
        extra = extra + gh_in[0, r - 1].astype(F32)
    pg_lo[...] = pack(extra, 0).astype(BF16)
    pg_hi[...] = pack(extra, 1).astype(BF16)

    def lead_back(p):
        return copy(pg_lo, gin_lo.at[p - 1], z_s.at[0], z_r.at[p - 1], (tm - p, head))

    def prev_back():
        return copy(pg_hi, gin_hi, z_s.at[1], z_r.at[3], (tm - 1, head))

    for p in range(1, SPAN):
        @pl.when(place == p)
        def _(p=p):
            lead_back(p).start()
            prev_back().start()

    for r in range(1, CROSS):
        k, arrival = ff_in(r)

        @pl.when(holds(k))
        def _(arrival=arrival):
            arrival.wait_recv()

    def region(j, tiles, first=0, rows=half_w):
        return gw_ref.at[
            pl.ds(pl.multiple_of(win_rows(j) + first, 16), rows), pl.ds(win_start(j), 128 * tiles)
        ]

    def at(d):
        return (pos + d + GROUP) % GROUP

    def peer_at(d):
        return (tm + (at(d) - pos) * stride, head)

    def hop(slot, j, d, tiles, first=0, rows=half_w):
        ref = region(j, tiles, first, rows)
        return copy(ref, ref, g_s.at[slot], g_r.at[slot], peer_at(d))

    half_r = half_w // 2
    near = (
        (0, 2, 0, half_r), (1, -2, half_r, half_r), (2, 2, half_r, half_r), (3, -2, 0, half_r),
        (4, 1, 0, half_w), (5, -1, 0, half_w),
    )
    onward = {
        0: ((6, -2, 2, 0, half_r), (7, -2, 1, 0, half_r)),
        1: ((8, 2, -2, half_r, half_r), (9, 2, -1, half_r, half_r)),
        2: ((10, -2, 1, half_r, half_r),),
        3: ((11, 2, -1, 0, half_r),),
    }

    def start(slot, j, *how):
        by_tiles(j, lambda tiles: hop(slot, j, how[0], tiles, *how[1:]).start())

    def arrived(slot, j, *how):
        by_tiles(j, lambda tiles: hop(slot, j, how[0], tiles, *how[1:]).wait_recv())

    def left(slot, j, *how):
        by_tiles(j, lambda tiles: hop(slot, j, how[0], tiles, *how[1:]).wait_send())

    for slot, *how in near:
        start(slot, pos, *how)
    for slot, d, *rows in near[:4]:
        arrived(slot, at(-d), d, *rows)
        for out, of, *how in onward[slot]:
            start(out, at(of), *how)

    for r in range(1, HEADS_AX):
        hh(r, 1).wait_recv()
    own = yt[1, head_rows(head), :].astype(F32)
    for r in range(1, HEADS_AX):
        own = own + gh_in[1, r - 1].astype(F32)

    @pl.when(place == 0)
    def _():
        for p in range(1, SPAN):
            copy(
                pg_lo, gin_lo.at[p - 1], z_s.at[0], z_r.at[p - 1], head_peer(1)
            ).wait_recv()

    @pl.when(place < SPAN - 1)
    def _():
        copy(pg_hi, gin_hi, z_s.at[1], z_r.at[3], head_peer(1)).wait_recv()

    lead_sum = gin_lo[0].astype(F32) + gin_lo[1].astype(F32) + gin_lo[2].astype(F32)
    lead_sum = jnp.where(place == 0, lead_sum, 0.0)
    prev_in = jnp.where(place < SPAN - 1, gin_hi[...].astype(F32), 0.0)
    local = jnp.where((place == 0) & low_lanes(own.shape), extra + roll_half(extra), 0.0)
    gh_ref[...] = (own + local + unpack(lead_sum, prev_in)).astype(BF16)

    for r in range(1, HEADS_AX):
        a1(r).wait_send()
        a3(r).wait_send()
        hh(r, 0).wait_send()
        hh(r, 1).wait_send()

    @pl.when(place == 0)
    def _():
        for p in range(1, SPAN):
            lead_out(p).wait_send()

    @pl.when(place < SPAN - 1)
    def _():
        prev_out().wait_send()

    @pl.when(place > 0)
    def _():
        lead_back(1).wait_send()
        prev_back().wait_send()

    for r in range(1, GROUP):
        by_tiles(group_pos(r), lambda tiles, r=r: fe(r, group_pos(r), tiles).wait_send())
        cc(r).wait_send()
    for slot, *how in near:
        left(slot, pos, *how)
    for r in range(1, CROSS):
        pl.when(holds(cross_pos(r)))(lambda r=r: ee(r).wait_send())

    @pl.when(holds(cross))
    def _():
        for r in range(1, CROSS):
            ff(r).wait_send()

    for slot, d, *rows in near[4:]:
        arrived(slot, at(-d), d, *rows)
    for sends in onward.values():
        for out, of, dist, *rows in sends:
            arrived(out, at(of - dist), dist, *rows)
    for sends in onward.values():
        for out, of, *how in sends:
            left(out, at(of), *how)


def hand_out(*refs):
    arrays, outs, held, sem = refs[:3], refs[3:6], refs[6:9], refs[9]
    arrivals, copies = [], []
    for i, chunks in ((1, 4), (0, 1), (2, 1)):
        rows = arrays[i].shape[0] // chunks
        for c in range(chunks):
            at, n = pl.ds(c * rows, rows), len(copies)
            arrivals.append(
                pltpu.make_async_copy(arrays[i].at[at], held[i].at[at], sem.at[0, n])
            )
            copies.append(pltpu.make_async_copy(held[i].at[at], outs[i].at[at], sem.at[1, n]))
    for arrival in arrivals:
        arrival.start()
    for arrival, out in zip(arrivals, copies):
        arrival.wait()
        out.start()
    for out in copies:
        out.wait()


def shards(hidden_states, w_query, w_key, w_value, grad_out):
    rows, width = hidden_states.shape
    full = w_query.shape[0]
    half = width // 2
    vm = pltpu.VMEM
    dma = pltpu.SemaphoreType.DMA
    scratch = [
        vm((full, rows), BF16),
        vm((full, rows), BF16),
        vm((3 * width, full), BF16),
        vm((width, rows), BF16),
        vm((half, 128), BF16), vm((half, 128), BF16),
        vm((half, 128), BF16), vm((half, 128), BF16),
        vm((3 * width, rows), BF16),
        vm((2 * width, rows), BF16),
        vm((2, rows, 2 * width), BF16),
        vm((width, rows), BF16),
        vm((GROUP, WIN, 128), BF16),
        vm((GROUP, half, 128), BF16),
        vm((CROSS, 32, 128), BF16),
        vm((CROSS - 1, 32, 128), BF16),
        vm((2, full, 128), BF16),
        vm((2, HEADS_AX - 1, width, 128), BF16),
        vm((half, 128), BF16), vm((half, 128), BF16),
        vm((SPAN - 1, half, 128), BF16), vm((half, 128), BF16),
        vm((2 * (width // HD), 256, 128), BF16),
        dma((5,)),
        dma((3,)), dma((3,)),
        dma((4,)), dma((2,)),
        dma((3,)), dma((3,)),
        dma((GROUP - 1,)), dma((GROUP - 1,)),
        dma((GROUP - 1,)), dma((GROUP - 1,)),
        dma((CROSS - 1,)), dma((CROSS - 1,)),
        dma((CROSS - 1,)), dma((CROSS - 1,)),
        dma((12,)), dma((12,)),
        dma((2, 3)), dma((2, 3)),
        dma((2,)), dma((4,)),
    ]
    att, gw, gh = pl.pallas_call(
        kernel,
        out_shape=(
            jax.ShapeDtypeStruct((width, rows), BF16),
            jax.ShapeDtypeStruct((width, full), BF16),
            jax.ShapeDtypeStruct((width, rows), BF16),
        ),
        in_specs=[pl.BlockSpec(memory_space=pltpu.HBM)] * 5,
        out_specs=[pl.BlockSpec(memory_space=pltpu.VMEM)] * 3,
        scratch_shapes=scratch,
        compiler_params=pltpu.CompilerParams(
            collective_id=0, has_side_effects=True, vmem_limit_bytes=60 * 2**20
        ),
    )(hidden_states.T, w_query.T, w_key.T, w_value.T, grad_out.T)
    att, gw, gh = pl.pallas_call(
        hand_out,
        out_shape=tuple(jax.ShapeDtypeStruct(a.shape, BF16) for a in (att, gw, gh)),
        in_specs=[pl.BlockSpec(memory_space=pltpu.HBM)] * 3,
        out_specs=[pl.BlockSpec(memory_space=pltpu.HBM)] * 3,
        scratch_shapes=[vm(a.shape, BF16) for a in (att, gw, gh)] + [dma((2, 6))],
        compiler_params=pltpu.CompilerParams(vmem_limit_bytes=60 * 2**20),
    )(att, gw, gh)
    return att.T, gw.T, gh.T


def solution(mesh):
    placed = (P("tm", "head"), P(None, "head"), P(None, "head"), P(None, "head"), P("tm", "head"))
    return jax.shard_map(
        shards,
        mesh=mesh,
        in_specs=placed,
        out_specs=(P("tm", "head"), P(None, "head"), P("tm", "head")),
        check_vma=False,
    )
```

```python
import functools

import jax
import jax.numpy as jnp
from jax import lax
from jax.experimental import pallas as pl
from jax.experimental.pallas import tpu as pltpu
from jax.sharding import PartitionSpec as P

MESH = pl.DeviceIdType.MESH
F32 = jnp.float32
BF16 = jnp.bfloat16

P_SIZE = 64
HD = 64
SPAN = 4
NZ = 8
GROUP = 8
CROSS = 16
HEADS_AX = 4
FAR_FIRST = sorted(range(1, GROUP), key=lambda r: abs(r - GROUP // 2))
CROSS_FAR_FIRST = sorted(range(1, CROSS), key=lambda r: abs(r - CROSS // 2))
WIN = 384
NT = (((1,), (1,)), ((), ()))


def mm(a, b):
    return jnp.dot(a, b, preferred_element_type=F32)


def mm_nt(a, b):
    return lax.dot_general(a, b, NT, preferred_element_type=F32)


def roll_half(x):
    return pltpu.roll(x, P_SIZE, 1)


def low_lanes(shape):
    return lax.broadcasted_iota(jnp.int32, shape, 1) < P_SIZE


def pack(tile, half):
    n = tile.shape[0] // 2
    top, bottom = tile[:n], tile[n:]
    low = low_lanes((n, 128))
    if half == 0:
        return jnp.where(low, top, roll_half(bottom))
    return jnp.where(low, roll_half(top), bottom)


def unpack(first, second):
    low = low_lanes(first.shape)
    return jnp.concatenate(
        [jnp.where(low, first, roll_half(second)), jnp.where(low, roll_half(first), second)], 0
    )


def kernel(
    hid_ref, wq_ref, wk_ref, wv_ref, go_ref,
    att_ref, gw_ref, gh_ref,
    xt, et, wt, gt, pk_lo, pk_hi, in_lo, in_hi,
    qkv, kve, kvn, dqt, fall, dqall, part, parts_in, yt, gh_in, pg_lo, pg_hi, gin_lo, gin_hi,
    pts, local_sem, a1_s, a1_r, a2_s, a2_r, a3_s, a3_r, fe_s, fe_r, c_s, c_r,
    e_s, e_r, f_s, f_r, g_s, g_r, h_s, h_r, z_s, z_r,
):
    tm = lax.axis_index("tm")
    head = lax.axis_index("head")
    core = head % 2
    z = tm % NZ
    xh = (tm // NZ) % 2
    y = tm // (2 * NZ)
    place = z % SPAN
    pos = (1 - core) * z + core * y
    stride = (1 - core) + core * 2 * NZ
    pos2 = (1 - core) * y + core * z
    stride2 = (1 - core) * 2 * NZ + core
    cross = pos2 * 2 + xh
    width = hid_ref.shape[0]
    half_w = width // 2

    def copy(src, dst, send, recv, device):
        return pltpu.make_async_remote_copy(
            src_ref=src, dst_ref=dst, send_sem=send, recv_sem=recv,
            device_id=device, device_id_type=MESH,
        )

    def head_peer(r):
        return (tm, (head + r) % HEADS_AX)

    def group_pos(r):
        return (pos + r) % GROUP

    def group_peer(r):
        return (tm + (group_pos(r) - pos) * stride, head)

    def cross_pos(r):
        return (cross + r) % CROSS

    def cross_peer(r):
        k = cross_pos(r)
        return (tm + (k // 2 - pos2) * stride2 + (k % 2 - xh) * NZ, head)

    def head_rows(h):
        return pl.ds(pl.multiple_of(h * width, 64), width)

    def is_wide(j):
        return (j // 2) % 2 == 0

    def by_tiles(j, run):
        pl.when(is_wide(j))(lambda: run(3))
        pl.when(jnp.logical_not(is_wide(j)))(lambda: run(2))

    def win_start(j):
        a = j // 2
        return pl.multiple_of(640 * (a // 2) + 384 * (a % 2), 128)

    def win_rows(j):
        return pl.multiple_of((j % 2) * half_w, 32)

    barrier = pltpu.get_barrier_semaphore()
    peers = (
        [head_peer(r) for r in range(1, HEADS_AX)]
        + [group_peer(r) for r in range(1, GROUP)]
        + [cross_peer(r) for r in range(1, CROSS)]
    )
    for peer in peers:
        pl.semaphore_signal(barrier, inc=1, device_id=peer, device_id_type=MESH)

    own_x = xt.at[head_rows(head)]
    loads = [
        pltpu.make_async_copy(hid_ref, own_x, local_sem.at[0]),
        pltpu.make_async_copy(wq_ref, wt.at[pl.ds(0, width)], local_sem.at[1]),
        pltpu.make_async_copy(wk_ref, wt.at[pl.ds(width, width)], local_sem.at[2]),
        pltpu.make_async_copy(wv_ref, wt.at[pl.ds(2 * width, width)], local_sem.at[3]),
        pltpu.make_async_copy(go_ref, gt, local_sem.at[4]),
    ]
    for load in loads:
        load.start()
    loads[0].wait()
    tile = xt[head_rows(head), :].astype(F32)
    pk_lo[...] = pack(tile, 0).astype(BF16)
    pk_hi[...] = pack(tile, 1).astype(BF16)
    pl.semaphore_wait(barrier, len(peers))

    def a1(r):
        return copy(own_x, own_x, a1_s.at[r - 1], a1_r.at[r - 1], head_peer(r))

    def a1_in(r):
        rows = xt.at[head_rows((head - r + HEADS_AX) % HEADS_AX)]
        return copy(rows, rows, a1_s.at[r - 1], a1_r.at[r - 1], head_peer(r))

    for r in range(1, HEADS_AX):
        a1(r).start()

    def lead_out(p):
        return copy(pk_lo, in_lo, a2_s.at[p - 1], a2_r.at[0], (tm + p, head))

    def prev_out():
        return copy(pk_hi, in_hi, a2_s.at[3], a2_r.at[1], (tm + 1, head))

    @pl.when(place == 0)
    def _():
        for p in reversed(range(1, SPAN)):
            lead_out(p).start()

    @pl.when(place < SPAN - 1)
    def _():
        prev_out().start()

    own_e = et.at[head_rows(head)]

    @pl.when(place == 0)
    def _():
        et[head_rows(head), :] = jnp.where(low_lanes(tile.shape), tile, roll_half(tile)).astype(BF16)

    @pl.when(place > 0)
    def _():
        copy(pk_lo, in_lo, a2_s.at[0], a2_r.at[0], (tm, (head + 1) % HEADS_AX)).wait_recv()
        copy(pk_hi, in_hi, a2_s.at[3], a2_r.at[1], (tm, (head + 1) % HEADS_AX)).wait_recv()
        et[head_rows(head), :] = unpack(in_lo[...].astype(F32), in_hi[...].astype(F32)).astype(BF16)

    def a3(r):
        return copy(own_e, own_e, a3_s.at[r - 1], a3_r.at[r - 1], head_peer(r))

    def a3_in(r):
        rows = et.at[head_rows((head - r + HEADS_AX) % HEADS_AX)]
        return copy(rows, rows, a3_s.at[r - 1], a3_r.at[r - 1], head_peer(r))

    for r in range(1, HEADS_AX):
        a3(r).start()
    for r in range(1, HEADS_AX):
        a1_in(r).wait_recv()

    def fe(r, j, tiles):
        return copy(
            xt.at[pl.ds(win_start(j), 128 * tiles)], fall.at[r, pl.ds(0, 128 * tiles)],
            fe_s.at[r - 1], fe_r.at[r - 1], group_peer(r),
        )

    for r in reversed(FAR_FIRST):
        by_tiles(group_pos(r), lambda tiles, r=r: fe(r, group_pos(r), tiles).start())

    @pl.when(is_wide(pos))
    def _():
        fall[0] = xt[pl.ds(win_start(pos), 384), :]

    @pl.when(jnp.logical_not(is_wide(pos)))
    def _():
        fall[0, 0:256] = xt[pl.ds(win_start(pos), 256), :]
        for r in range(GROUP):
            fall[r, 256:384] = jnp.zeros((128, 128), BF16)

    for load in loads[1:]:
        load.wait()
    qkv[...] = mm(wt[...], xt[...]).astype(BF16)
    kvn[1] = jnp.transpose(qkv[width:, :])
    for r in range(1, HEADS_AX):
        a3_in(r).wait_recv()
    kve[...] = mm(wt[width:, :], et[...]).astype(BF16)
    kvn[0] = jnp.transpose(kve[...])

    scale = HD ** (-0.5)
    low = low_lanes((P_SIZE, 128))
    zero = jnp.zeros((P_SIZE, 128), BF16)
    heads_here = width // HD

    def spread(lead, second, index):
        pts[index, 0:64, :] = lead
        pts[index, 64:128, :] = jnp.where(low, second, zero)
        pts[index, 128:192, :] = jnp.where(low, zero, second)
        pts[index, 192:256, :] = zero

    def cc(r):
        return copy(
            dqt.at[pl.ds(win_rows(group_pos(r)), half_w)], dqall.at[r],
            c_s.at[r - 1], c_r.at[r - 1], group_peer(r),
        )

    for i in range(heads_here):
        a, b = HD * i, HD * (i + 1)
        q = qkv[a:b, :]
        cot = gt[a:b, :]
        k_extra, k_own = kvn[0, :, a:b], kvn[1, 0:64, a:b]
        v_extra, v_own = kvn[0, :, width + a : width + b], kvn[1, 0:64, width + a : width + b]
        s_extra, s_own = mm(k_extra, q) * scale, mm(k_own, q) * scale
        s_lead, s_second = s_extra[:64], jnp.where(low, s_extra[64:], s_own)
        top = jnp.maximum(
            jnp.max(s_lead, 0, keepdims=True), jnp.max(s_second, 0, keepdims=True)
        )
        e_lead, e_second = jnp.exp(s_lead - top), jnp.exp(s_second - top)
        inv = 1.0 / (jnp.sum(e_lead, 0, keepdims=True) + jnp.sum(e_second, 0, keepdims=True))
        p_lead, p_second = e_lead * inv, e_second * inv
        d_extra, d_own = mm(v_extra, cot), mm(v_own, cot)
        d_lead, d_second = d_extra[:64], jnp.where(low, d_extra[64:], d_own)
        inner = jnp.sum(p_lead * d_lead, 0, keepdims=True) + jnp.sum(
            p_second * d_second, 0, keepdims=True
        )
        spread(
            (p_lead * (d_lead - inner) * scale).astype(BF16),
            (p_second * (d_second - inner) * scale).astype(BF16),
            2 * i,
        )
        spread(p_lead.astype(BF16), p_second.astype(BF16), 2 * i + 1)
        k_wide = jnp.concatenate([kve[a:b, :], qkv[width + a : width + b, :]], 1)
        dqt[a:b, :] = mm(k_wide, pts[2 * i]).astype(BF16)
    for r in FAR_FIRST:
        cc(r).start()
    dqall[0] = dqt[pl.ds(win_rows(pos), half_w), :]


    dks, dvs = [], []
    for i in range(heads_here):
        a, b = HD * i, HD * (i + 1)
        v_wide = jnp.concatenate(
            [kve[width + a : width + b, :], qkv[2 * width + a : 2 * width + b, :]], 1
        )
        att_ref[a:b, :] = mm(v_wide, pts[2 * i + 1]).astype(BF16)
        dks.append(mm_nt(qkv[a:b, :], pts[2 * i]).astype(BF16))
        dvs.append(mm_nt(gt[a:b, :], pts[2 * i + 1]).astype(BF16))

    for r in range(1, GROUP):
        by_tiles(pos, lambda tiles, r=r: fe(r, pos, tiles).wait_recv())
    near_blocks, far_blocks = (0, 1, 7, 2), (6, 3, 5, 4)

    def products(blocks):
        for r in blocks:
            if r:
                cc(r).wait_recv()
        return mm_nt(
            jnp.concatenate([dqall[r] for r in blocks], 1),
            jnp.concatenate([fall[r] for r in blocks], 1),
        )

    window = products(near_blocks)
    window = (window + products(far_blocks)).astype(BF16)
    for k in range(15):
        i, l = k // 3, k % 3
        part[k] = window[32 * i : 32 * i + 32, 128 * l : 128 * l + 128]

    def holds(k):
        return (k < 15) & (is_wide(pos) | (k % 3 < 2))

    def ee(r):
        return copy(
            part.at[cross_pos(r)], parts_in.at[r - 1], e_s.at[r - 1], e_r.at[r - 1], cross_peer(r)
        )

    for r in CROSS_FAR_FIRST:
        pl.when(holds(cross_pos(r)))(lambda r=r: ee(r).start())

    dk_n = jnp.transpose(jnp.concatenate(dks, 0))
    dv_n = jnp.transpose(jnp.concatenate(dvs, 0))
    dq_n = jnp.transpose(dqt[...])

    def hh(r, part):
        return copy(
            yt.at[part, head_rows((head + r) % HEADS_AX)], gh_in.at[part, r - 1],
            h_s.at[part, r - 1], h_r.at[part, r - 1], head_peer(r),
        )

    for c in range(5):
        cols = slice(256 * c, 256 * (c + 1))
        terms = mm(dk_n[:128], wt[width : 2 * width, cols]) + mm(dv_n[:128], wt[2 * width :, cols])
        yt[0, cols, :] = jnp.transpose(terms.astype(BF16))
    for r in range(1, HEADS_AX):
        hh(r, 0).start()

    def piece(k):
        return gw_ref.at[
            pl.ds(pl.multiple_of(win_rows(pos) + 32 * (k // 3), 32), 32),
            pl.ds(pl.multiple_of(win_start(pos) + 128 * (k % 3), 128), 128),
        ]

    def ff(r):
        return copy(piece(cross), piece(cross), f_s.at[r - 1], f_r.at[r - 1], cross_peer(r))

    def ff_in(r):
        k = (cross - r + CROSS) % CROSS
        return k, copy(piece(k), piece(k), f_s.at[r - 1], f_r.at[r - 1], cross_peer(r))

    @pl.when(holds(cross))
    def _():
        total = part[cross].astype(F32)
        for r in reversed(CROSS_FAR_FIRST):
            ee(r).wait_recv()
            total = total + parts_in[r - 1].astype(F32)
        gw_ref[
            pl.ds(pl.multiple_of(win_rows(pos) + 32 * (cross // 3), 32), 32),
            pl.ds(pl.multiple_of(win_start(pos) + 128 * (cross % 3), 128), 128),
        ] = total.astype(BF16)
        for r in CROSS_FAR_FIRST:
            ff(r).start()

    for c in range(5):
        cols = slice(256 * c, 256 * (c + 1))
        terms = mm(dk_n[128:], wt[width : 2 * width, cols]) + mm(dv_n[128:], wt[2 * width :, cols])
        terms = terms + mm(dq_n, wt[0:width, cols])
        yt[1, cols, :] = jnp.transpose(terms.astype(BF16))

    for r in range(1, HEADS_AX):
        hh(r, 1).start()
    for r in range(1, HEADS_AX):
        hh(r, 0).wait_recv()
    extra = yt[0, head_rows(head), :].astype(F32)
    for r in range(1, HEADS_AX):
        extra = extra + gh_in[0, r - 1].astype(F32)
    pg_lo[...] = pack(extra, 0).astype(BF16)
    pg_hi[...] = pack(extra, 1).astype(BF16)

    def lead_back(p):
        return copy(pg_lo, gin_lo.at[p - 1], z_s.at[0], z_r.at[p - 1], (tm - p, head))

    def prev_back():
        return copy(pg_hi, gin_hi, z_s.at[1], z_r.at[3], (tm - 1, head))

    for p in range(1, SPAN):
        @pl.when(place == p)
        def _(p=p):
            lead_back(p).start()
            prev_back().start()

    for r in range(1, CROSS):
        k, arrival = ff_in(r)

        @pl.when(holds(k))
        def _(arrival=arrival):
            arrival.wait_recv()

    def region(j, tiles, first=0, rows=half_w):
        return gw_ref.at[
            pl.ds(pl.multiple_of(win_rows(j) + first, 16), rows), pl.ds(win_start(j), 128 * tiles)
        ]

    def at(d):
        return (pos + d + GROUP) % GROUP

    def peer_at(d):
        return (tm + (at(d) - pos) * stride, head)

    def hop(slot, j, d, tiles, first=0, rows=half_w):
        ref = region(j, tiles, first, rows)
        return copy(ref, ref, g_s.at[slot], g_r.at[slot], peer_at(d))

    half_r = half_w // 2
    near = (
        (0, 2, 0, half_r), (1, -2, half_r, half_r), (2, 2, half_r, half_r), (3, -2, 0, half_r),
        (4, 1, 0, half_w), (5, -1, 0, half_w),
    )
    onward = {
        0: ((6, -2, 2, 0, half_r), (7, -2, 1, 0, half_r)),
        1: ((8, 2, -2, half_r, half_r), (9, 2, -1, half_r, half_r)),
        2: ((10, -2, 1, half_r, half_r),),
        3: ((11, 2, -1, 0, half_r),),
    }

    def start(slot, j, *how):
        by_tiles(j, lambda tiles: hop(slot, j, how[0], tiles, *how[1:]).start())

    def arrived(slot, j, *how):
        by_tiles(j, lambda tiles: hop(slot, j, how[0], tiles, *how[1:]).wait_recv())

    def left(slot, j, *how):
        by_tiles(j, lambda tiles: hop(slot, j, how[0], tiles, *how[1:]).wait_send())

    for slot, *how in near:
        start(slot, pos, *how)
    for slot, d, *rows in near[:4]:
        arrived(slot, at(-d), d, *rows)
        for out, of, *how in onward[slot]:
            start(out, at(of), *how)

    for r in range(1, HEADS_AX):
        hh(r, 1).wait_recv()
    own = yt[1, head_rows(head), :].astype(F32)
    for r in range(1, HEADS_AX):
        own = own + gh_in[1, r - 1].astype(F32)

    @pl.when(place == 0)
    def _():
        for p in range(1, SPAN):
            copy(
                pg_lo, gin_lo.at[p - 1], z_s.at[0], z_r.at[p - 1], head_peer(1)
            ).wait_recv()

    @pl.when(place < SPAN - 1)
    def _():
        copy(pg_hi, gin_hi, z_s.at[1], z_r.at[3], head_peer(1)).wait_recv()

    lead_sum = gin_lo[0].astype(F32) + gin_lo[1].astype(F32) + gin_lo[2].astype(F32)
    lead_sum = jnp.where(place == 0, lead_sum, 0.0)
    prev_in = jnp.where(place < SPAN - 1, gin_hi[...].astype(F32), 0.0)
    local = jnp.where((place == 0) & low_lanes(own.shape), extra + roll_half(extra), 0.0)
    gh_ref[...] = (own + local + unpack(lead_sum, prev_in)).astype(BF16)

    for r in range(1, HEADS_AX):
        a1(r).wait_send()
        a3(r).wait_send()
        hh(r, 0).wait_send()
        hh(r, 1).wait_send()

    @pl.when(place == 0)
    def _():
        for p in range(1, SPAN):
            lead_out(p).wait_send()

    @pl.when(place < SPAN - 1)
    def _():
        prev_out().wait_send()

    @pl.when(place > 0)
    def _():
        lead_back(1).wait_send()
        prev_back().wait_send()

    for r in range(1, GROUP):
        by_tiles(group_pos(r), lambda tiles, r=r: fe(r, group_pos(r), tiles).wait_send())
        cc(r).wait_send()
    for slot, *how in near:
        left(slot, pos, *how)
    for r in range(1, CROSS):
        pl.when(holds(cross_pos(r)))(lambda r=r: ee(r).wait_send())

    @pl.when(holds(cross))
    def _():
        for r in range(1, CROSS):
            ff(r).wait_send()

    for slot, d, *rows in near[4:]:
        arrived(slot, at(-d), d, *rows)
    for sends in onward.values():
        for out, of, dist, *rows in sends:
            arrived(out, at(of - dist), dist, *rows)
    for sends in onward.values():
        for out, of, *how in sends:
            left(out, at(of), *how)


def hand_out(*refs):
    arrays, outs, held, sem = refs[:3], refs[3:6], refs[6:9], refs[9]
    arrivals, copies = [], []
    for i, chunks in ((1, 4), (0, 1), (2, 1)):
        rows = arrays[i].shape[0] // chunks
        for c in range(chunks):
            at, n = pl.ds(c * rows, rows), len(copies)
            arrivals.append(
                pltpu.make_async_copy(arrays[i].at[at], held[i].at[at], sem.at[0, n])
            )
            copies.append(pltpu.make_async_copy(held[i].at[at], outs[i].at[at], sem.at[1, n]))
    for arrival in arrivals:
        arrival.start()
    for arrival, out in zip(arrivals, copies):
        arrival.wait()
        out.start()
    for out in copies:
        out.wait()


def shards(hidden_states, w_query, w_key, w_value, grad_out):
    rows, width = hidden_states.shape
    full = w_query.shape[0]
    half = width // 2
    vm = pltpu.VMEM
    dma = pltpu.SemaphoreType.DMA
    scratch = [
        vm((full, rows), BF16),
        vm((full, rows), BF16),
        vm((3 * width, full), BF16),
        vm((width, rows), BF16),
        vm((half, 128), BF16), vm((half, 128), BF16),
        vm((half, 128), BF16), vm((half, 128), BF16),
        vm((3 * width, rows), BF16),
        vm((2 * width, rows), BF16),
        vm((2, rows, 2 * width), BF16),
        vm((width, rows), BF16),
        vm((GROUP, WIN, 128), BF16),
        vm((GROUP, half, 128), BF16),
        vm((CROSS, 32, 128), BF16),
        vm((CROSS - 1, 32, 128), BF16),
        vm((2, full, 128), BF16),
        vm((2, HEADS_AX - 1, width, 128), BF16),
        vm((half, 128), BF16), vm((half, 128), BF16),
        vm((SPAN - 1, half, 128), BF16), vm((half, 128), BF16),
        vm((2 * (width // HD), 256, 128), BF16),
        dma((5,)),
        dma((3,)), dma((3,)),
        dma((4,)), dma((2,)),
        dma((3,)), dma((3,)),
        dma((GROUP - 1,)), dma((GROUP - 1,)),
        dma((GROUP - 1,)), dma((GROUP - 1,)),
        dma((CROSS - 1,)), dma((CROSS - 1,)),
        dma((CROSS - 1,)), dma((CROSS - 1,)),
        dma((12,)), dma((12,)),
        dma((2, 3)), dma((2, 3)),
        dma((2,)), dma((4,)),
    ]
    att, gw, gh = pl.pallas_call(
        kernel,
        out_shape=(
            jax.ShapeDtypeStruct((width, rows), BF16),
            jax.ShapeDtypeStruct((width, full), BF16),
            jax.ShapeDtypeStruct((width, rows), BF16),
        ),
        in_specs=[pl.BlockSpec(memory_space=pltpu.HBM)] * 5,
        out_specs=[pl.BlockSpec(memory_space=pltpu.VMEM)] * 3,
        scratch_shapes=scratch,
        compiler_params=pltpu.CompilerParams(
            collective_id=0, has_side_effects=True, vmem_limit_bytes=60 * 2**20
        ),
    )(hidden_states.T, w_query.T, w_key.T, w_value.T, grad_out.T)
    att, gw, gh = pl.pallas_call(
        hand_out,
        out_shape=tuple(jax.ShapeDtypeStruct(a.shape, BF16) for a in (att, gw, gh)),
        in_specs=[pl.BlockSpec(memory_space=pltpu.HBM)] * 3,
        out_specs=[pl.BlockSpec(memory_space=pltpu.HBM)] * 3,
        scratch_shapes=[vm(a.shape, BF16) for a in (att, gw, gh)] + [dma((2, 6))],
        compiler_params=pltpu.CompilerParams(vmem_limit_bytes=60 * 2**20),
    )(att, gw, gh)
    return att.T, gw.T, gh.T


def solution(mesh):
    placed = (P("tm", "head"), P(None, "head"), P(None, "head"), P(None, "head"), P("tm", "head"))
    return jax.shard_map(
        shards,
        mesh=mesh,
        in_specs=placed,
        out_specs=(P("tm", "head"), P(None, "head"), P("tm", "head")),
        check_vma=False,
    )
```
